32 devices in a mesh: expert: 8 (over z, x), tensor: 4 (over y, core).
Axes of the slice: x: 2, y: 2, z: 4, core: 2. Of those that a mesh axis runs over, the one named last changes fastest.
Arguments:
- tokens: bfloat16 [4096, 768], P('expert'), may hold values from -6 to 6
- norm_first: bfloat16 [768], replicated, may hold values from 0.5 to 1.5
- w_query: bfloat16 [768, 768], P(None, 'tensor'), may hold values from -0.078125 to 0.078125
- w_key: bfloat16 [768, 768], P(None, 'tensor'), may hold values from -0.078125 to 0.078125
- w_value: bfloat16 [768, 768], P(None, 'tensor'), may hold values from -0.21875 to 0.21875
- w_output: bfloat16 [768, 768], P('tensor'), may hold values from -0.875 to 0.875
- bias_table: bfloat16 [32, 12], P(None, 'tensor'), may hold values from -4 to 4
- norm_second: bfloat16 [768], replicated, may hold values from 0.5 to 1.5
- w_router: bfloat16 [768, 8], replicated, may hold values from -0.15625 to 0.15625
- w_expert_in: bfloat16 [8, 768, 3072], P('expert', None, 'tensor'), may hold values from -0.21875 to 0.21875
- w_expert_out: bfloat16 [8, 3072, 768], P('expert', 'tensor'), may hold values from -0.625 to 0.625
- routes: int32 [4096, 1], P('expert'), may hold values from 0 to 7; in each aligned block of 512 rows (0 to 511, 512 to 1023, ...) at most 96 rows name the same one
- cotangent: bfloat16 [4096, 768], P('expert'), may hold values from -6 to 6
Outputs:
- layer_out: bfloat16 [4096, 768], P('expert')
- grad_tokens: float32 [4096, 768], P('expert')
- grad_norm_first: float32 [768], replicated
- grad_w_query: float32 [768, 768], P('expert', 'tensor')
- grad_w_key: float32 [768, 768], P('expert', 'tensor')
- grad_w_value: float32 [768, 768], P('expert', 'tensor')
- grad_w_output: float32 [768, 768], P('tensor', 'expert')
- grad_bias_table: float32 [32, 12], P(None, 'tensor')
- grad_norm_second: float32 [768], replicated
- grad_w_router: float32 [768, 8], replicated
- grad_w_expert_in: float32 [8, 768, 3072], P('expert', None, 'tensor')
- grad_w_expert_out: float32 [8, 3072, 768], P('expert', 'tensor')
The draws below stay inside these ranges and needn't reach their ends.
Inputs may be any that keep to these rules, and one draw needn't show every extreme that they name: `routes`: in each aligned block of 512 tokens no expert is named by more than 96 tokens, a bound that some block reaches.
All inputs are finite; a program needn't handle non-finite values.
Results may differ from the reference program's by a relative error of at most 0.014.
Values may be sent and summed in bfloat16 or wider, within the bound.
No kernel may reach another device: no remote copies, remote signals or barrier semaphores. Data moves between devices by JAX's collectives and lax.ppermute only.
A program may use at most 128 MiB of HBM per device.

```python
import math
import jax
import jax.numpy as jnp
import numpy as np
from jax import lax

D = 768
HEADS = 12
DH = 64
FF = 3072
BUCKETS = 32
LEN = 512
TOK_DEV = 512
TOKENS = 4096
EXPERTS = 8
SLOT = 96
N_EXPERT = 8


def strengthened(entries, stream_key, source, target, blocks, factor):
    def block_of(dim):
        return (jnp.arange(entries.shape[dim]) // (entries.shape[dim] // blocks)).reshape((-1,) + (1,) * (entries.ndim - 1 - dim))

    one_side = jax.random.permutation(stream_key, blocks)[block_of(target)]
    far = (block_of(target) + blocks // 2) % blocks
    return jnp.where((block_of(source) == one_side) | (block_of(source) == far), factor * entries, entries)


def block_levels(key, extent, cuts, low, high):
    def one(dim, blocks):
        heights = jax.random.uniform(jax.random.fold_in(jax.random.fold_in(key, 6), dim), (blocks,), jnp.float32, low / len(cuts), high / len(cuts))
        return jnp.repeat(jnp.exp(heights), extent[dim] // blocks).reshape((-1,) + (1,) * (len(extent) - dim - 1))

    gain = one(*cuts[0])
    for cut in cuts[1:]:
        gain = gain * one(*cut)
    return gain


def routed_block(key, own, number, rows, amount, top, reach, slope):
    order = jax.random.permutation(key, amount)
    crowded, usual = shares(amount, rows * top, reach, slope, True), shares(amount, rows * top, reach, slope, False)
    places = jnp.arange(amount)

    def named(sizes, rotation):
        used = int((sizes > 0).sum())
        fixed = max(1, used // 4)
        passed = fixed + (places - fixed + rotation * (used - fixed)) % max(1, amount - fixed)
        return jnp.zeros((amount,), jnp.int32).at[order[jnp.where(places < fixed, places, passed)]].set(jnp.asarray(sizes, jnp.int32))

    sizes = jnp.where(number % 4 == 0, named(crowded, number // 4), named(usual, number - number // 4 - 1))
    mixed = jax.random.permutation(jax.random.fold_in(own, 3), amount)
    source_of, taker = mixed[0:amount // 2 * 2:2], mixed[1:amount // 2 * 2:2]
    slack = jnp.minimum(sizes[source_of] - 1, reach - sizes[taker]) // 2
    slack = jnp.where((source_of == order[0]) | (taker == order[0]) | (sizes[taker] == 0), 0, jnp.maximum(slack, 0))
    passed = jax.random.randint(jax.random.fold_in(own, 4), (amount // 2,), 0, 1 << 20) % (slack + 1)
    sizes = sizes.at[source_of].add(-passed).at[taker].add(passed)
    labels = jnp.searchsorted(jnp.cumsum(sizes), jnp.arange(rows * top), side="right").astype(jnp.int32)
    listing = labels.reshape(top, rows).T
    listing = listing[jax.random.permutation(jax.random.fold_in(own, 1), rows)]
    rotation = jax.random.randint(jax.random.fold_in(own, 2), (rows, 1), 0, top)
    return jnp.take_along_axis(listing, (jnp.arange(top)[None, :] + rotation) % top, axis=1)


def shares(amount, total, bound, slope, full):
    loads = [(1 << 20) // math.isqrt(grade ** slope) + 1 for grade in range(1, amount + 1)]
    largest = bound if full else min(bound, max(-(-total // amount), total * loads[0] // sum(loads)))
    least = 1 if total - largest >= amount - 1 else 0
    holding, rest = [largest] + [least] * (amount - 1), total - largest - least * (amount - 1)
    while rest > 0:
        free = [i for i in range(1, amount) if holding[i] < largest] or [i for i in range(1, amount) if holding[i] < bound]
        whole, left = sum([loads[i] for i in free]), rest
        for i in free:
            more = min(bound - holding[i], max(1, left * loads[i] // whole), rest)
            holding[i] = holding[i] + more
            rest = rest - more
    return np.array(holding)


def scatter_about(stream_key, shape, scale, bound, split=(), kind=jnp.bfloat16):
    values = jax.random.normal(stream_key, shape, jnp.float32) * scale
    if len(split) > 0:
        values = block_levels(stream_key, shape, split, -0.22, 0.18) * values
    return jnp.clip(values, min=-bound, max=bound).astype(kind)


def bell_draw_with(own_key, extent, spread, reach, cuts, heavy, kind=jnp.bfloat16):
    array = spread * jax.random.normal(own_key, extent, jnp.float32)
    if cuts:
        array = array * block_levels(own_key, extent, cuts, -0.22, 0.18)
    return jnp.clip(strengthened(array, jax.random.fold_in(own_key, 3), *heavy), -reach, reach).astype(kind)


def setup_inputs(seed: int = 0) -> dict:
    splits = jax.random.split(jax.random.key(seed), 14)
    tokens = scatter_about(splits[0], (TOKENS, D), 1.0, 6.0, ((0, 8),))
    norm_first = jnp.clip(1.0 + 0.1 * jax.random.normal(splits[1], (D,), jnp.float32), 0.5, 1.5).astype(jnp.bfloat16)
    w_query = scatter_about(splits[2], (D, HEADS * DH), (8 * D) ** -0.5, 0.078125, ((1, 4),))
    w_key = scatter_about(splits[3], (D, HEADS * DH), (8 * D) ** -0.5, 0.078125, ((1, 4),))
    w_value = scatter_about(splits[4], (D, HEADS * DH), D ** -0.5, 0.21875, ((1, 4),))
    w_output = scatter_about(splits[5], (HEADS * DH, D), (HEADS * DH // 16) ** -0.5, 0.875, ((0, 4),))
    bias_table = scatter_about(splits[6], (BUCKETS, HEADS), 1.0, 4.0, ((1, 4),))
    norm_second = jnp.clip(1.0 + 0.1 * jax.random.normal(splits[7], (D,), jnp.float32), 0.5, 1.5).astype(jnp.bfloat16)
    w_router = scatter_about(splits[8], (D, EXPERTS), (2 * D) ** -0.5, 0.15625)
    w_expert_in = scatter_about(splits[9], (EXPERTS, D, FF), D ** -0.5, 0.21875, ((0, 8), (2, 4)))
    w_expert_out = scatter_about(splits[10], (EXPERTS, FF, D), (max(1, 2 * FF // (EXPERTS * EXPERTS))) ** -0.5, 0.625, ((0, 8), (1, 4)))
    routes_keys = jax.random.split(jax.random.fold_in(splits[11], 1), TOKENS // TOK_DEV)
    routes_turns = jax.random.permutation(jax.random.fold_in(splits[11], 3), TOKENS // TOK_DEV)
    routes = jax.vmap(lambda own, number: routed_block(jax.random.fold_in(splits[11], 2), own, number, TOK_DEV, EXPERTS, 1, SLOT, 2))(routes_keys, routes_turns).reshape((TOKENS, 1))
    cotangent = bell_draw_with(splits[12], (TOKENS, D), 1.0, 6.0, ((0, 8),), (0, 1, 8, 2.0))
    return dict(tokens=tokens, norm_first=norm_first, w_query=w_query, w_key=w_key, w_value=w_value, w_output=w_output, bias_table=bias_table, norm_second=norm_second, w_router=w_router, w_expert_in=w_expert_in, w_expert_out=w_expert_out, routes=routes, cotangent=cotangent)


EPSILON = 1e-06
HIGHEST = lax.Precision.HIGHEST
THRESHOLDS = (12, 16, 23, 32, 46, 64, 91)

@jax.custom_vjp
def low(v):
    return lax.optimization_barrier(v.astype(jnp.bfloat16)).astype(jnp.float32)

@jax.custom_vjp
def low_back(v):
    return v

def low_keep(v):
    return (low(v), None)

def low_pass(kept, grad):
    return (grad,)

def back_keep(v):
    return (v, None)

def back_low(kept, grad):
    return (low(grad),)
low.defvjp(low_keep, low_pass)
low_back.defvjp(back_keep, back_low)

def rounded(values):
    return low_back(low(values))

def bucket_ids(length):
    positions = jnp.arange(length, dtype=jnp.int32)
    relative = positions[None, :] - positions[:, None]
    distance = jnp.abs(relative)
    beyond = jnp.full_like(distance, 8)
    for threshold in THRESHOLDS:
        beyond = beyond + (distance >= threshold).astype(jnp.int32)
    bucket_index = jnp.where(distance < 8, distance, beyond)
    return bucket_index + 16 * (relative > 0).astype(jnp.int32)

def rms_norm(values, gain_vector):
    inv_rms = lax.rsqrt(lax.optimization_barrier(jnp.mean(values * values, axis=-1, keepdims=True)) + EPSILON)
    return values * inv_rms * gain_vector

def layer(inputs, gain_first, w_query, w_key, w_value, w_output, table_values, gain_second, w_router, w_expert_in, w_expert_out, route_hot, position):
    normed = low(rms_norm(inputs, gain_first))
    bias_map = jnp.transpose(table_values[bucket_ids(LEN)], (2, 0, 1))
    total_seqs = TOKENS // LEN
    per_step = math.gcd(total_seqs, max(1, 4096 // LEN))
    split_shape = (per_step, LEN, HEADS, DH)

    def attend(seq_block):
        queries = rounded(jnp.dot(seq_block, w_query, precision=HIGHEST)).reshape(split_shape)
        key_rows = rounded(jnp.dot(seq_block, w_key, precision=HIGHEST)).reshape(split_shape)
        value_rows = rounded(jnp.dot(seq_block, w_value, precision=HIGHEST)).reshape(split_shape)
        scores = low_back(jnp.einsum('gqhd,gkhd->ghqk', queries, key_rows, precision=HIGHEST) + bias_map[None])
        weights = low(jax.nn.softmax(scores, axis=-1))
        mixed_rows = jnp.einsum('ghqk,gkhd->gqhd', weights, value_rows, precision=HIGHEST)
        return rounded(mixed_rows).reshape(per_step * LEN, HEADS * DH)
    blocks = normed.reshape(total_seqs // per_step, per_step * LEN, D)
    mixed_all = lax.map(jax.checkpoint(attend), blocks).reshape(TOKENS, HEADS * DH)
    hidden = inputs + low_back(jnp.dot(mixed_all, w_output, precision=HIGHEST))
    normed_second = low(rms_norm(hidden, gain_second))
    router_probs = jax.nn.softmax(jnp.dot(normed_second, w_router, precision=HIGHEST), axis=-1)
    gating = lax.optimization_barrier(jnp.sum(router_probs * route_hot, axis=-1))
    buffer = jnp.zeros((EXPERTS * N_EXPERT * SLOT, D), jnp.float32).at[position].set(normed_second)
    buffer = low_back(buffer).reshape(EXPERTS, N_EXPERT * SLOT, D)

    def expert(packed):
        expert_rows, weight_in, weight_out = packed
        pre_act = low_back(jnp.dot(expert_rows, weight_in, precision=HIGHEST))
        active = low(jax.nn.gelu(pre_act, approximate=True))
        return rounded(jnp.dot(active, weight_out, precision=HIGHEST))
    results = lax.map(jax.checkpoint(expert), (buffer, w_expert_in, w_expert_out)).reshape(EXPERTS * N_EXPERT * SLOT, D)
    returned = results[position]
    return hidden + gating[:, None] * returned

def reference(tokens, norm_first, w_query, w_key, w_value, w_output, bias_table, norm_second, w_router, w_expert_in, w_expert_out, routes, cotangent):
    chosen = routes[:, 0].astype(jnp.int32)
    route_count = (chosen[:, None] == jnp.arange(EXPERTS, dtype=jnp.int32)[None, :]).astype(jnp.int32)
    blocked = route_count.reshape(N_EXPERT, TOK_DEV, EXPERTS)
    earlier = (jnp.cumsum(blocked, axis=1) - blocked).reshape(TOKENS, EXPERTS)
    slot_index = lax.optimization_barrier(jnp.sum(earlier * route_count, axis=1)).astype(jnp.int32)
    source = jnp.arange(TOKENS, dtype=jnp.int32) // TOK_DEV
    position = (chosen * (N_EXPERT * SLOT) + source * SLOT + slot_index).astype(jnp.int32)
    route_hot = route_count.astype(jnp.float32)

    def closed(inputs, gain_first, query_weight, key_weight, value_weight, output_weight, table_values, gain_second, router_weight, expert_in, expert_out):
        return layer(inputs, gain_first, query_weight, key_weight, value_weight, output_weight, table_values, gain_second, router_weight, expert_in, expert_out, route_hot, position)
    result, pullback = jax.vjp(closed, tokens.astype(jnp.float32), norm_first.astype(jnp.float32), w_query.astype(jnp.float32), w_key.astype(jnp.float32), w_value.astype(jnp.float32), w_output.astype(jnp.float32), bias_table.astype(jnp.float32), norm_second.astype(jnp.float32), w_router.astype(jnp.float32), w_expert_in.astype(jnp.float32), w_expert_out.astype(jnp.float32))
    gradients = pullback(cotangent.astype(jnp.float32))
    return (result.astype(jnp.bfloat16), gradients[0], gradients[1], gradients[2], gradients[3], gradients[4], gradients[5], gradients[6], gradients[7], gradients[8], gradients[9], gradients[10])
```

```python
import jax
import jax.numpy as jnp
from jax import lax
from jax.sharding import PartitionSpec as P

BUCKETS = 32
LEN = 512
TENSOR = 4

EPSILON = 1e-06
THRESHOLDS = (12, 16, 23, 32, 46, 64, 91)
BF16 = jnp.bfloat16
F32 = jnp.float32


def dot(left, right):
    return jnp.dot(left, right, preferred_element_type=F32)


def dot_t(left, right):
    return lax.dot_general(left, right, (((1,), (1,)), ((), ())), preferred_element_type=F32)


def t_dot(left, right):
    return lax.dot_general(left, right, (((0,), (0,)), ((), ())), preferred_element_type=F32)


def bucket_ids(length):
    positions = jnp.arange(length, dtype=jnp.int32)
    relative = positions[None, :] - positions[:, None]
    distance = jnp.abs(relative)
    beyond = jnp.full_like(distance, 8)
    for threshold in THRESHOLDS:
        beyond = beyond + (distance >= threshold).astype(jnp.int32)
    bucket_index = jnp.where(distance < 8, distance, beyond)
    return bucket_index + 16 * (relative > 0).astype(jnp.int32)


def inv_rms_of(values):
    return lax.rsqrt(jnp.mean(values * values, axis=-1, keepdims=True) + EPSILON)


def rms_norm_back(values, inv_rms, gain, grad):
    scaled = gain * grad
    inner = jnp.mean(scaled * values, axis=-1, keepdims=True)
    return inv_rms * scaled - values * (inv_rms * inv_rms * inv_rms * inner)


def gelu_tanh(values):
    return jax.nn.gelu(values, approximate=True)


def swap(values, axis, mask):
    size = lax.axis_size(axis)
    return lax.ppermute(values, axis, [(i, i ^ mask) for i in range(size)])


def gather_tensor(values):
    far = swap(values, "tensor", 2)
    near = swap(values, "tensor", 1)
    return values, near, far, swap(far, "tensor", 1)


def exchange_expert(blocks, relative):
    count = blocks.shape[0]
    if not relative:
        return lax.all_to_all(blocks, "expert", split_axis=0, concat_axis=0, tiled=True)
    arrived = [blocks[0]]
    for mask in range(1, count):
        arrived.append(swap(blocks[mask], "expert", mask))
    return jnp.stack(arrived)


def scatter_sum_tensor(parts):
    sent = jnp.concatenate([parts[1], parts[3]]).astype(BF16)
    got = swap(sent, "tensor", 1).astype(F32)
    rows = parts[0].shape[0]
    own = parts[0] + got[:rows]
    other = (parts[2] + got[rows:]).astype(BF16)
    return (own + swap(other, "tensor", 2).astype(F32)).astype(BF16)


def sum_tensor(part, index):
    half = part.shape[0] // 2
    low, high = part[:half], part[half:]
    is_high = (index & 1) == 1
    sent = jnp.where(is_high, low, high).astype(BF16)
    kept = jnp.where(is_high, high, low)
    pair = (kept + swap(sent, "tensor", 1).astype(F32)).astype(BF16)
    total = (pair.astype(F32) + swap(pair, "tensor", 2).astype(F32)).astype(BF16)
    other = swap(total, "tensor", 1)
    return jnp.concatenate([jnp.where(is_high, other, total), jnp.where(is_high, total, other)]).astype(F32)


def scatter_sum_expert(part, index):
    count = lax.axis_size("expert")
    rows = part.shape[0] // count
    if count != 8:
        return lax.psum_scatter(part, "expert", scatter_dimension=0, tiled=True)
    blocks = part.reshape(count // 2, 2, rows, part.shape[1])
    first = index & 1
    sent = jnp.where(first == 1, blocks[:, 0], blocks[:, 1]).astype(BF16)
    kept = jnp.where(first == 1, blocks[:, 1], blocks[:, 0])
    pair = kept + swap(sent, "expert", 1).astype(F32)
    place = index >> 1
    total = lax.dynamic_index_in_dim(pair, place, 0, keepdims=False)
    low = pair.astype(BF16)
    for mask in (1, 2, 3):
        total = total + swap(
            lax.dynamic_index_in_dim(low, place ^ mask, 0, keepdims=False), "expert", 2 * mask
        ).astype(F32)
    return total


def sum_all(values):
    for axis in ("tensor", "expert"):
        mask = 1
        while mask < lax.axis_size(axis):
            values = values + swap(values, axis, mask)
            mask = 2 * mask
    return values


def on_device(
    tokens,
    norm_first,
    w_query,
    w_key,
    w_value,
    w_output,
    bias_table,
    norm_second,
    w_router,
    w_expert_in,
    w_expert_out,
    routes,
    cotangent,
):
    tok_rows, width = tokens.shape
    experts = w_router.shape[1]
    capacity = max(2, 3 * tok_rows // (2 * experts))
    quarter = -(-capacity // TENSOR)
    relative = experts == 8
    heads_here = bias_table.shape[1]
    head_size = w_query.shape[1] // heads_here
    columns = heads_here * head_size
    seq_shape = (tok_rows, heads_here, head_size)
    my_tensor = lax.axis_index("tensor")
    my_expert = lax.axis_index("expert")
    inputs = tokens.astype(F32)
    gain_first = norm_first.astype(F32)
    gain_second = norm_second.astype(F32)
    upstream = cotangent.astype(F32)
    weight_in = w_expert_in[0]
    weight_out = w_expert_out[0]

    inv_first = inv_rms_of(inputs)
    normed = (inputs * inv_first * gain_first).astype(BF16)
    w_qkv = jnp.concatenate([w_query, w_key, w_value], axis=1)
    qkv = dot(normed, w_qkv).astype(BF16)
    queries = qkv[:, :columns].reshape(seq_shape)
    key_rows = qkv[:, columns : 2 * columns].reshape(seq_shape)
    value_rows = qkv[:, 2 * columns :].reshape(seq_shape)
    bucket_hot = (
        jnp.arange(BUCKETS, dtype=jnp.int32)[:, None] == bucket_ids(LEN).reshape(1, LEN * LEN)
    ).astype(BF16)
    bias_map = dot(bias_table.T, bucket_hot).reshape(heads_here, LEN, LEN)
    scores = jnp.einsum("qhd,khd->hqk", queries, key_rows, preferred_element_type=F32) + bias_map
    row_max = jnp.max(scores, axis=-1, keepdims=True)
    exponent = jnp.exp(scores - row_max)
    probs = exponent / jnp.sum(exponent, axis=-1, keepdims=True)
    weights = probs.astype(BF16)
    mixed = jnp.einsum("hqk,khd->qhd", weights, value_rows, preferred_element_type=F32)
    mixed = mixed.astype(BF16).reshape(tok_rows, columns)

    chosen = routes[:, 0]
    route_hot = chosen[:, None] == jnp.arange(experts, dtype=jnp.int32)[None, :]
    places = jnp.arange(tok_rows, dtype=jnp.int32)
    before = (places[:, None] > places[None, :]).astype(BF16)
    earlier = dot(before, route_hot.astype(BF16))
    slot_index = jnp.sum(jnp.where(route_hot, earlier, 0.0), axis=1).astype(jnp.int32)
    chunk = (slot_index // quarter) ^ my_tensor
    target = chosen ^ my_expert if relative else chosen
    place = (chunk * experts + target) * quarter + slot_index % quarter
    chunk_rows = experts * quarter
    place_hot = (
        place[:, None] == jnp.arange(TENSOR * chunk_rows, dtype=jnp.int32)[None, :]
    ).astype(BF16)

    mixed_parts = gather_tensor(mixed)
    output_parts = gather_tensor(w_output)
    attn = [dot(rows, part) for rows, part in zip(mixed_parts, output_parts)]
    hidden = inputs + ((attn[0] + attn[1]) + (attn[2] + attn[3]))
    inv_second = inv_rms_of(hidden)
    normed_second = (hidden * inv_second * gain_second).astype(BF16)
    router_probs = jax.nn.softmax(dot(normed_second, w_router), axis=-1)
    gating = jnp.sum(jnp.where(route_hot, router_probs, 0.0), axis=-1, keepdims=True)
    grad_returned = (upstream * gating).astype(BF16)

    def dispatch(rows):
        own = t_dot(place_hot[:, :chunk_rows], rows).astype(BF16)
        blocks = exchange_expert(own.reshape(experts, quarter, width), relative)
        return jnp.concatenate(gather_tensor(blocks.reshape(chunk_rows, width)))

    def send_home(part):
        own = scatter_sum_tensor([part[i * chunk_rows : (i + 1) * chunk_rows] for i in range(TENSOR)])
        blocks = exchange_expert(own.reshape(experts, quarter, width), relative)
        return dot(place_hot, jnp.concatenate(gather_tensor(blocks.reshape(chunk_rows, width))))

    expert_rows = dispatch(normed_second)
    grad_rows = dispatch(grad_returned)

    pre_act = dot(expert_rows, weight_in)
    activated, gelu_pull = jax.vjp(gelu_tanh, pre_act)
    active = activated.astype(BF16)
    grad_active = dot_t(grad_rows, weight_out)
    grad_pre = gelu_pull(grad_active)[0].astype(BF16)
    gate_grad = jnp.sum(active.astype(F32) * grad_active, axis=1, keepdims=True)
    row_probs = jax.nn.softmax(dot(expert_rows, w_router), axis=-1)
    own_hot = (jnp.arange(experts, dtype=jnp.int32) == my_expert).astype(F32)[None, :]
    grad_logits = (gate_grad * (own_hot - row_probs)).astype(BF16)
    back_part = dot_t(grad_pre, weight_in) + dot_t(grad_logits, w_router)
    grad_normed_second = send_home(back_part)
    returned = send_home(dot(active, weight_out))
    layer_out = (hidden + gating * returned).astype(BF16)
    grad_expert_out = t_dot(active, grad_rows)[None]
    grad_expert_in = t_dot(expert_rows, grad_pre)[None]
    router_part = t_dot(grad_logits, expert_rows)

    norm_second_part = jnp.sum(grad_normed_second * hidden * inv_second, axis=0, keepdims=True)
    grad_hidden = upstream + rms_norm_back(hidden, inv_second, gain_second, grad_normed_second)
    grad_attn = grad_hidden.astype(BF16)
    output_part = t_dot(grad_attn, mixed)
    grad_mixed = dot_t(grad_attn, w_output).astype(BF16).reshape(seq_shape)

    value_back = jnp.einsum("hqk,qhd->khd", weights, grad_mixed, preferred_element_type=F32)
    probs_grad = jnp.einsum("qhd,khd->hqk", grad_mixed, value_rows, preferred_element_type=F32)
    inner_sum = jnp.sum(probs_grad * probs, axis=-1, keepdims=True)
    score_grad = (probs * (probs_grad - inner_sum)).astype(BF16)
    query_back = jnp.einsum("hqk,khd->qhd", score_grad, key_rows, preferred_element_type=F32)
    key_back = jnp.einsum("hqk,qhd->khd", score_grad, queries, preferred_element_type=F32)
    bias_part = jnp.einsum(
        "hp,bp->bh",
        score_grad.reshape(heads_here, LEN * LEN),
        bucket_hot,
        preferred_element_type=F32,
    )
    qkv_back = jnp.concatenate(
        [rows.astype(BF16).reshape(tok_rows, columns) for rows in (query_back, key_back, value_back)],
        axis=1,
    )
    qkv_part = t_dot(normed, qkv_back)
    normed_part = dot_t(qkv_back, w_qkv)
    normed_back = sum_tensor(normed_part, my_tensor)
    norm_first_part = jnp.sum(normed_part * inputs * inv_first, axis=0, keepdims=True)
    grad_tokens = grad_hidden + rms_norm_back(inputs, inv_first, gain_first, normed_back)

    grad_output = scatter_sum_expert(output_part, my_expert).T
    grad_qkv = scatter_sum_expert(qkv_part, my_expert)
    bias_size = BUCKETS * heads_here
    bias_row = jnp.where(
        (jnp.arange(TENSOR * bias_size, dtype=jnp.int32) // bias_size == my_tensor)[None, :],
        jnp.tile(bias_part.reshape(1, bias_size), (1, TENSOR)),
        0.0,
    )
    bias_row = jnp.pad(bias_row, ((0, 0), (0, width - TENSOR * bias_size)))
    small = sum_all(
        jnp.concatenate(
            [router_part, jnp.where(my_tensor == 0, norm_second_part, 0.0), norm_first_part, bias_row]
        )
    )
    grad_router = small[:experts].T
    grad_bias = lax.dynamic_slice(small[experts + 2], (my_tensor * bias_size,), (bias_size,))
    return (
        layer_out,
        grad_tokens,
        small[experts + 1],
        grad_qkv[:, :columns],
        grad_qkv[:, columns : 2 * columns],
        grad_qkv[:, 2 * columns :],
        grad_output,
        grad_bias.reshape(BUCKETS, heads_here),
        small[experts],
        grad_router,
        grad_expert_in,
        grad_expert_out,
    )


def solution(mesh):
    return jax.shard_map(
        on_device,
        mesh=mesh,
        in_specs=(
            P("expert", None),
            P(),
            P(None, "tensor"),
            P(None, "tensor"),
            P(None, "tensor"),
            P("tensor", None),
            P(None, "tensor"),
            P(),
            P(),
            P("expert", None, "tensor"),
            P("expert", "tensor", None),
            P("expert", None),
            P("expert", None),
        ),
        out_specs=(
            P("expert", None),
            P("expert", None),
            P(),
            P("expert", "tensor"),
            P("expert", "tensor"),
            P("expert", "tensor"),
            P("tensor", "expert"),
            P(None, "tensor"),
            P(),
            P(),
            P("expert", None, "tensor"),
            P("expert", "tensor", None),
        ),
        check_vma=False,
    )
```

```python
import functools

import jax
import jax.numpy as jnp
from jax import lax
from jax.experimental import pallas as pl
from jax.experimental.pallas import tpu as pltpu
from jax.sharding import PartitionSpec as P

BUCKETS = 32
LEN = 512
TENSOR = 4

EPSILON = 1e-06
THRESHOLDS = (12, 16, 23, 32, 46, 64, 91)
BF16 = jnp.bfloat16
F32 = jnp.float32
VMEM_LIMIT = 48 * 1024 * 1024


def dot(left, right):
    return jnp.dot(left, right, preferred_element_type=F32)


def dot_t(left, right):
    return lax.dot_general(left, right, (((1,), (1,)), ((), ())), preferred_element_type=F32)


def t_dot(left, right):
    return lax.dot_general(left, right, (((0,), (0,)), ((), ())), preferred_element_type=F32)


def inv_rms_of(values):
    return lax.rsqrt(jnp.mean(values * values, axis=-1, keepdims=True) + EPSILON)


def rms_norm_back(values, inv_rms, gain, grad):
    scaled = gain * grad
    inner = jnp.mean(scaled * values, axis=-1, keepdims=True)
    return inv_rms * scaled - values * (inv_rms * inv_rms * inv_rms * inner)


def gelu_tanh(values):
    return jax.nn.gelu(values, approximate=True)


TILE = 128


def bias_tiles(table_ref, head):
    row = lax.broadcasted_iota(jnp.int32, (TILE, TILE), 0)
    col = lax.broadcasted_iota(jnp.int32, (TILE, TILE), 1)
    tiles = []
    for offset in (-1, 0, 1):
        shift = col - row + offset * TILE
        distance = jnp.abs(shift)

        def chain(base):
            tile = jnp.full((TILE, TILE), table_ref[base, head], F32)
            for n in range(1, 8):
                tile = jnp.where(distance >= n, table_ref[base + n, head], tile)
            for n, threshold in enumerate((8,) + THRESHOLDS):
                tile = jnp.where(distance >= threshold, table_ref[base + 8 + n, head], tile)
            return tile

        if offset < 0:
            tiles.append(chain(0))
        elif offset > 0:
            tiles.append(chain(16))
        else:
            tiles.append(jnp.where(shift > 0, chain(16), chain(0)))
    return tiles


def bias_rows(table_ref, tiles, head, block):
    parts = []
    for other in range(LEN // TILE):
        offset = other - block
        if offset < -1:
            parts.append(jnp.full((TILE, TILE), table_ref[15, head], F32))
        elif offset > 1:
            parts.append(jnp.full((TILE, TILE), table_ref[31, head], F32))
        else:
            parts.append(tiles[offset + 1])
    return jnp.concatenate(parts, axis=1)


def head_columns(values, head, size):
    lane = lax.broadcasted_iota(jnp.int32, values.shape, 1)
    return jnp.where((lane >= head * size) & (lane < (head + 1) * size), values, jnp.zeros_like(values))


def attend_kernel(heads, size, table_ref, tokens_ref, gain_ref, wq_ref, wk_ref, wv_ref, normed_ref, q_ref, k_ref, v_ref, mixed_ref, total_ref):
    values = tokens_ref[...].astype(F32)
    normed = (values * inv_rms_of(values) * gain_ref[...].astype(F32)).astype(BF16)
    normed_ref[...] = normed
    q_ref[...] = dot(normed, wq_ref[...]).astype(BF16)
    k_ref[...] = dot(normed, wk_ref[...]).astype(BF16)
    v_ref[...] = dot(normed, wv_ref[...]).astype(BF16)
    all_tiles = [bias_tiles(table_ref, head) for head in range(heads)]
    keys = k_ref[...]
    head_values = [head_columns(v_ref[...], head, size) for head in range(heads)]
    for block in range(LEN // TILE):
        rows = pl.ds(block * TILE, TILE)
        queries = q_ref[rows, :]
        mixed = None
        lane = lax.broadcasted_iota(jnp.int32, (TILE, TILE), 1)
        totals = jnp.zeros((TILE, TILE), F32)
        for head in range(heads):
            scores = dot_t(head_columns(queries, head, size), keys)
            scores = scores + bias_rows(table_ref, all_tiles[head], head, block)
            row_max = jnp.max(scores, axis=-1, keepdims=True)
            exponent = jnp.exp(scores - row_max)
            row_total = jnp.sum(exponent, axis=-1, keepdims=True)
            weights = (exponent * (1.0 / row_total)).astype(BF16)
            part = dot(weights, head_values[head])
            mixed = part if mixed is None else mixed + part
            totals = jnp.where(lane == head, row_max + jnp.log(row_total), totals)
        mixed_ref[rows, :] = mixed.astype(BF16)
        total_ref[rows, :] = totals


def attend(tokens, gain, w_query, w_key, w_value, table, heads):
    rows, columns = tokens.shape[0], w_query.shape[1]
    small = jax.ShapeDtypeStruct((rows, columns), BF16)
    vmem = pl.BlockSpec(memory_space=pltpu.VMEM)
    return pl.pallas_call(
        functools.partial(attend_kernel, heads, columns // heads),
        out_shape=(
            jax.ShapeDtypeStruct(tokens.shape, BF16), small, small, small, small,
            jax.ShapeDtypeStruct((rows, TILE), F32),
        ),
        in_specs=[pl.BlockSpec(memory_space=pltpu.SMEM)] + [vmem] * 5,
        out_specs=(vmem,) * 6,
        compiler_params=pltpu.CompilerParams(vmem_limit_bytes=VMEM_LIMIT),
        cost_estimate=pl.CostEstimate(flops=rows * 768 * 576 * 2 + 4 * rows * rows * 192, bytes_accessed=5_000_000, transcendentals=heads * rows * rows),
        name="attend",
    )(table, tokens, gain, w_query, w_key, w_value)


def attend_back_kernel(heads, size, table_ref, q_ref, k_ref, v_ref, total_ref, grad_ref, qb_ref, kb_ref, vb_ref, bias_ref, kacc, vacc):
    keys, all_values = k_ref[...], v_ref[...]
    kacc[...] = jnp.zeros_like(kacc)
    vacc[...] = jnp.zeros_like(vacc)
    all_tiles = [bias_tiles(table_ref, head) for head in range(heads)]
    head_keys = [head_columns(keys, head, size) for head in range(heads)]
    count = LEN // TILE
    near = [[None] * 3 for _ in range(heads)]
    far = [[None] * 2 for _ in range(heads)]
    for block in range(count):
        rows = pl.ds(block * TILE, TILE)
        queries, grads, totals = q_ref[rows, :], grad_ref[rows, :], total_ref[rows, :]
        query_back = None
        key_back = value_back = None
        for head in range(heads):
            head_queries = head_columns(queries, head, size)
            head_grads = head_columns(grads, head, size)
            scores = dot_t(head_queries, keys)
            scores = scores + bias_rows(table_ref, all_tiles[head], head, block)
            probs = jnp.exp(scores - totals[:, head : head + 1])
            probs_grad = dot_t(head_grads, all_values)
            inner = jnp.sum(probs_grad * probs, axis=-1, keepdims=True)
            score_grad = (probs * (probs_grad - inner)).astype(BF16)
            part = dot(score_grad, head_keys[head])
            query_back = part if query_back is None else query_back + part
            kacc[...] += t_dot(score_grad, head_queries)
            vacc[...] += t_dot(probs.astype(BF16), head_grads)
            wide = score_grad.astype(F32)
            for other in range(count):
                offset = other - block
                tile = wide[:, other * TILE : (other + 1) * TILE]
                if abs(offset) <= 1:
                    held = near[head][offset + 1]
                    near[head][offset + 1] = tile if held is None else held + tile
                else:
                    side = 0 if offset < 0 else 1
                    summed = jnp.sum(tile.reshape(TILE // 8, 8, TILE), axis=0)
                    held = far[head][side]
                    far[head][side] = summed if held is None else held + summed
        qb_ref[rows, :] = query_back.astype(BF16)
    kb_ref[...] = kacc[...].astype(BF16)
    vb_ref[...] = vacc[...].astype(BF16)
    row = lax.broadcasted_iota(jnp.int32, (TILE, TILE), 0)
    col = lax.broadcasted_iota(jnp.int32, (TILE, TILE), 1)

    def fold(values):
        return jnp.sum(values.reshape(TILE // 8, 8, TILE), axis=0)

    steps = tuple(range(8)) + (8,) + THRESHOLDS
    edges = steps + (1 << 20,)
    pieces = []
    for head in range(heads):
        for sign in (0, 1):
            for n in range(16):
                piece = None
                for offset in ((-1, 0) if sign == 0 else (0, 1)):
                    low = 0 if offset == 0 else 1
                    if edges[n + 1] <= low or edges[n] > (TILE - 1 if offset == 0 else 2 * TILE - 1):
                        continue
                    shift = col - row + offset * TILE
                    distance = jnp.abs(shift)
                    inside = (distance >= edges[n]) & (distance < edges[n + 1])
                    if offset == 0:
                        inside = inside & ((shift > 0) if sign else (shift <= 0))
                    found = fold(jnp.where(inside, near[head][offset + 1], 0.0))
                    piece = found if piece is None else piece + found
                if n == 15:
                    piece = piece + far[head][sign]
                if piece is None:
                    piece = jnp.zeros((8, TILE), F32)
                pieces.append(jnp.sum(piece, axis=0, keepdims=True))
    table = jnp.concatenate(pieces, axis=0)
    bias_ref[...] = jnp.broadcast_to(jnp.sum(table, axis=1, keepdims=True), bias_ref.shape)


def attend_back(queries, keys, values, totals, grad_mixed, table, heads):
    rows, columns = queries.shape
    small = jax.ShapeDtypeStruct((rows, columns), BF16)
    vmem = pl.BlockSpec(memory_space=pltpu.VMEM)
    return pl.pallas_call(
        functools.partial(attend_back_kernel, heads, columns // heads),
        out_shape=(small, small, small, jax.ShapeDtypeStruct((heads * BUCKETS, TILE), F32)),
        in_specs=[pl.BlockSpec(memory_space=pltpu.SMEM)] + [vmem] * 5,
        out_specs=(vmem,) * 4,
        scratch_shapes=[pltpu.VMEM((rows, columns), F32), pltpu.VMEM((rows, columns), F32)],
        compiler_params=pltpu.CompilerParams(vmem_limit_bytes=VMEM_LIMIT),
        cost_estimate=pl.CostEstimate(flops=10 * rows * rows * 192, bytes_accessed=2_000_000, transcendentals=heads * rows * rows),
        name="attend_back",
    )(table, queries, keys, values, totals, grad_mixed)


def swap(values, axis, mask):
    size = lax.axis_size(axis)
    return lax.ppermute(values, axis, [(i, i ^ mask) for i in range(size)])


def gather_tensor(values):
    far = swap(values, "tensor", 2)
    near = swap(values, "tensor", 1)
    return values, near, far, swap(far, "tensor", 1)


def exchange_expert(blocks):
    return lax.all_to_all(blocks, "expert", split_axis=0, concat_axis=0, tiled=True)


def scatter_sum_tensor(parts):
    sent = jnp.concatenate([parts[1], parts[3]]).astype(BF16)
    got = swap(sent, "tensor", 1).astype(F32)
    rows = parts[0].shape[0]
    own = parts[0] + got[:rows]
    other = (parts[2] + got[rows:]).astype(BF16)
    return (own + swap(other, "tensor", 2).astype(F32)).astype(BF16)


def sum_tensor(part, index):
    half = part.shape[0] // 2
    low, high = part[:half], part[half:]
    is_high = (index & 1) == 1
    sent = jnp.where(is_high, low, high).astype(BF16)
    kept = jnp.where(is_high, high, low)
    pair = (kept + swap(sent, "tensor", 1).astype(F32)).astype(BF16)
    total = (pair.astype(F32) + swap(pair, "tensor", 2).astype(F32)).astype(BF16)
    other = swap(total, "tensor", 1)
    return jnp.concatenate([jnp.where(is_high, other, total), jnp.where(is_high, total, other)]).astype(F32)


def scatter_sum_expert(part, index):
    count = lax.axis_size("expert")
    rows = part.shape[0] // count
    if count != 8:
        return lax.psum_scatter(part, "expert", scatter_dimension=0, tiled=True)
    blocks = part.reshape(count // 2, 2, rows, part.shape[1])
    first = index & 1
    sent = jnp.where(first == 1, blocks[:, 0], blocks[:, 1]).astype(BF16)
    kept = jnp.where(first == 1, blocks[:, 1], blocks[:, 0])
    pair = kept + swap(sent, "expert", 1).astype(F32)
    place = index >> 1
    total = lax.dynamic_index_in_dim(pair, place, 0, keepdims=False)
    low = pair.astype(BF16)
    for mask in (1, 2, 3):
        total = total + swap(
            lax.dynamic_index_in_dim(low, place ^ mask, 0, keepdims=False), "expert", 2 * mask
        ).astype(F32)
    return total


def sum_all(values):
    for axis in ("tensor", "expert"):
        mask = 1
        while mask < lax.axis_size(axis):
            values = values + swap(values, axis, mask)
            mask = 2 * mask
    return values


def on_device(
    tokens,
    norm_first,
    w_query,
    w_key,
    w_value,
    w_output,
    bias_table,
    norm_second,
    w_router,
    w_expert_in,
    w_expert_out,
    routes,
    cotangent,
):
    tok_rows, width = tokens.shape
    experts = w_router.shape[1]
    capacity = max(2, 3 * tok_rows // (2 * experts))
    quarter = -(-capacity // TENSOR)
    heads_here = bias_table.shape[1]
    columns = w_query.shape[1]
    my_tensor = lax.axis_index("tensor")
    my_expert = lax.axis_index("expert")
    inputs = tokens.astype(F32)
    gain_first = norm_first.astype(F32)
    gain_second = norm_second.astype(F32)
    upstream = cotangent.astype(F32)
    weight_in = w_expert_in[0]
    weight_out = w_expert_out[0]

    table = bias_table.astype(F32)
    normed, queries, key_rows, value_rows, mixed, totals = attend(
        tokens, norm_first.reshape(1, width), w_query, w_key, w_value, table, heads_here
    )
    inv_first = inv_rms_of(inputs)

    chosen = routes[:, 0]
    route_hot = chosen[:, None] == jnp.arange(experts, dtype=jnp.int32)[None, :]
    places = jnp.arange(tok_rows, dtype=jnp.int32)
    before = (places[:, None] > places[None, :]).astype(BF16)
    earlier = dot(before, route_hot.astype(BF16))
    slot_index = jnp.sum(jnp.where(route_hot, earlier, 0.0), axis=1).astype(jnp.int32)
    chunk = (slot_index // quarter) ^ my_tensor
    place = (chunk * experts + chosen) * quarter + slot_index % quarter
    chunk_rows = experts * quarter
    place_hot = (
        place[:, None] == jnp.arange(TENSOR * chunk_rows, dtype=jnp.int32)[None, :]
    ).astype(BF16)

    mixed_parts = gather_tensor(mixed)
    output_parts = gather_tensor(w_output)
    attn = [dot(rows, part) for rows, part in zip(mixed_parts, output_parts)]
    hidden = inputs + ((attn[0] + attn[1]) + (attn[2] + attn[3]))
    inv_second = inv_rms_of(hidden)
    normed_second = (hidden * inv_second * gain_second).astype(BF16)
    router_probs = jax.nn.softmax(dot(normed_second, w_router), axis=-1)
    gating = jnp.sum(jnp.where(route_hot, router_probs, 0.0), axis=-1, keepdims=True)
    grad_returned = (upstream * gating).astype(BF16)

    both = jnp.concatenate([normed_second, grad_returned], axis=1)
    own = t_dot(place_hot[:, :chunk_rows], both).astype(BF16)
    arrived = exchange_expert(own.reshape(experts, quarter, 2 * width)).reshape(chunk_rows, 2 * width)
    expert_rows = jnp.concatenate(gather_tensor(arrived[:, :width]))
    grad_rows = jnp.concatenate(gather_tensor(arrived[:, width:]))

    def send_home(part):
        own = scatter_sum_tensor([part[i * chunk_rows : (i + 1) * chunk_rows] for i in range(TENSOR)])
        blocks = exchange_expert(own.reshape(experts, quarter, width))
        return dot(place_hot, jnp.concatenate(gather_tensor(blocks.reshape(chunk_rows, width))))

    pre_act = dot(expert_rows, weight_in)
    activated, gelu_pull = jax.vjp(gelu_tanh, pre_act)
    active = activated.astype(BF16)
    grad_active = dot_t(grad_rows, weight_out)
    grad_pre = gelu_pull(grad_active)[0].astype(BF16)
    gate_grad = jnp.sum(active.astype(F32) * grad_active, axis=1, keepdims=True)
    row_probs = jax.nn.softmax(dot(expert_rows, w_router), axis=-1)
    own_hot = (jnp.arange(experts, dtype=jnp.int32) == my_expert).astype(F32)[None, :]
    grad_logits = (gate_grad * (own_hot - row_probs)).astype(BF16)
    back_part = dot_t(grad_pre, weight_in) + dot_t(grad_logits, w_router)
    grad_normed_second = send_home(back_part)
    returned = send_home(dot(active, weight_out))
    layer_out = (hidden + gating * returned).astype(BF16)
    grad_expert_out = t_dot(active, grad_rows)[None]
    grad_expert_in = t_dot(expert_rows, grad_pre)[None]
    router_part = t_dot(grad_logits, expert_rows)

    norm_second_part = jnp.sum(grad_normed_second * hidden * inv_second, axis=0, keepdims=True)
    grad_hidden = upstream + rms_norm_back(hidden, inv_second, gain_second, grad_normed_second)
    grad_attn = grad_hidden.astype(BF16)
    output_part = t_dot(grad_attn, mixed)
    grad_mixed = dot_t(grad_attn, w_output).astype(BF16)

    query_back, key_back, value_back, bias_part = attend_back(
        queries, key_rows, value_rows, totals, grad_mixed, table, heads_here
    )
    bias_part = bias_part[:, 0].reshape(heads_here, BUCKETS).T
    qkv_back = jnp.concatenate([query_back, key_back, value_back], axis=1)
    w_qkv = jnp.concatenate([w_query, w_key, w_value], axis=1)
    qkv_part = t_dot(normed, qkv_back)
    normed_part = dot_t(qkv_back, w_qkv)
    normed_back = sum_tensor(normed_part, my_tensor)
    norm_first_part = jnp.sum(normed_part * inputs * inv_first, axis=0, keepdims=True)
    grad_tokens = grad_hidden + rms_norm_back(inputs, inv_first, gain_first, normed_back)

    grad_output = scatter_sum_expert(output_part, my_expert).T
    grad_qkv = scatter_sum_expert(qkv_part, my_expert)
    bias_size = BUCKETS * heads_here
    bias_row = jnp.where(
        (jnp.arange(TENSOR * bias_size, dtype=jnp.int32) // bias_size == my_tensor)[None, :],
        jnp.tile(bias_part.reshape(1, bias_size), (1, TENSOR)),
        0.0,
    )
    bias_row = jnp.pad(bias_row, ((0, 0), (0, width - TENSOR * bias_size)))
    small = sum_all(
        jnp.concatenate(
            [router_part, jnp.where(my_tensor == 0, norm_second_part, 0.0), norm_first_part, bias_row]
        )
    )
    grad_router = small[:experts].T
    grad_bias = lax.dynamic_slice(small[experts + 2], (my_tensor * bias_size,), (bias_size,))
    return (
        layer_out,
        grad_tokens,
        small[experts + 1],
        grad_qkv[:, :columns],
        grad_qkv[:, columns : 2 * columns],
        grad_qkv[:, 2 * columns :],
        grad_output,
        grad_bias.reshape(BUCKETS, heads_here),
        small[experts],
        grad_router,
        grad_expert_in,
        grad_expert_out,
    )


def solution(mesh):
    return jax.shard_map(
        on_device,
        mesh=mesh,
        in_specs=(
            P("expert", None),
            P(),
            P(None, "tensor"),
            P(None, "tensor"),
            P(None, "tensor"),
            P("tensor", None),
            P(None, "tensor"),
            P(),
            P(),
            P("expert", None, "tensor"),
            P("expert", "tensor", None),
            P("expert", None),
            P("expert", None),
        ),
        out_specs=(
            P("expert", None),
            P("expert", None),
            P(),
            P("expert", "tensor"),
            P("expert", "tensor"),
            P("expert", "tensor"),
            P("tensor", "expert"),
            P(None, "tensor"),
            P(),
            P(),
            P("expert", None, "tensor"),
            P("expert", "tensor", None),
        ),
        check_vma=False,
    )
```

```python
import functools

import jax
import jax.numpy as jnp
from jax import lax
from jax.experimental import pallas as pl
from jax.experimental.pallas import tpu as pltpu
from jax.sharding import PartitionSpec as P

BUCKETS = 32
LEN = 512
TENSOR = 4

EPSILON = 1e-06
THRESHOLDS = (12, 16, 23, 32, 46, 64, 91)
BF16 = jnp.bfloat16
F32 = jnp.float32
GELU_SCALE = (2.0 / 3.141592653589793) ** 0.5
GELU_CUBE = 0.044715
MIB = 1024 * 1024


def dot(left, right):
    return jnp.dot(left, right, preferred_element_type=F32)


def dot_t(left, right):
    return lax.dot_general(left, right, (((1,), (1,)), ((), ())), preferred_element_type=F32)


def t_dot(left, right):
    return lax.dot_general(left, right, (((0,), (0,)), ((), ())), preferred_element_type=F32)


def inv_rms_of(values):
    return lax.rsqrt(jnp.mean(values * values, axis=-1, keepdims=True) + EPSILON)


def rms_norm_back(values, inv_rms, gain, grad):
    scaled = gain * grad
    inner = jnp.mean(scaled * values, axis=-1, keepdims=True)
    return inv_rms * scaled - values * (inv_rms * inv_rms * inv_rms * inner)


TILE = 128


def bias_tiles(table_ref, head):
    row = lax.broadcasted_iota(jnp.int32, (TILE, TILE), 0)
    col = lax.broadcasted_iota(jnp.int32, (TILE, TILE), 1)
    tiles = []
    for offset in (-1, 0, 1):
        shift = col - row + offset * TILE
        distance = jnp.abs(shift)

        def chain(base):
            tile = jnp.full((TILE, TILE), table_ref[head, base], F32)
            for n in range(1, 8):
                tile = jnp.where(distance >= n, table_ref[head, base + n], tile)
            for n, threshold in enumerate((8,) + THRESHOLDS):
                tile = jnp.where(distance >= threshold, table_ref[head, base + 8 + n], tile)
            return tile

        if offset < 0:
            tiles.append(chain(0))
        elif offset > 0:
            tiles.append(chain(16))
        else:
            tiles.append(jnp.where(shift > 0, chain(16), chain(0)))
    return tiles


def bias_rows(table_ref, tiles, head, block):
    parts = []
    for other in range(LEN // TILE):
        offset = other - block
        if offset < -1:
            parts.append(jnp.full((TILE, TILE), table_ref[head, 15], F32))
        elif offset > 1:
            parts.append(jnp.full((TILE, TILE), table_ref[head, 31], F32))
        else:
            parts.append(tiles[offset + 1])
    return jnp.concatenate(parts, axis=1)


def head_columns(values, head, size):
    lane = lax.broadcasted_iota(jnp.int32, values.shape, 1)
    return jnp.where((lane >= head * size) & (lane < (head + 1) * size), values, jnp.zeros_like(values))


def attend_kernel(heads, size, table_ref, tokens_ref, gain_ref, wq_ref, wk_ref, wv_ref, normed_ref, q_ref, k_ref, v_ref, mixed_ref, total_ref):
    values = tokens_ref[...].astype(F32)
    normed = (values * inv_rms_of(values) * gain_ref[0:1, :]).astype(BF16)
    normed_ref[...] = normed
    normed_ref.leave()
    q_ref[...] = dot_t(normed, wq_ref[...]).astype(BF16)
    q_ref.leave()
    k_ref[...] = dot_t(normed, wk_ref[...]).astype(BF16)
    k_ref.leave()
    v_ref[...] = dot_t(normed, wv_ref[...]).astype(BF16)
    v_ref.leave()
    all_tiles = [bias_tiles(table_ref, head) for head in range(heads)]
    keys = k_ref[...]
    head_values = [head_columns(v_ref[...], head, size) for head in range(heads)]
    for block in range(LEN // TILE):
        rows = pl.ds(block * TILE, TILE)
        queries = q_ref[rows, :]
        mixed = None
        lane = lax.broadcasted_iota(jnp.int32, (TILE, TILE), 1)
        totals = jnp.zeros((TILE, TILE), F32)
        for head in range(heads):
            scores = dot_t(head_columns(queries, head, size), keys)
            scores = scores + bias_rows(table_ref, all_tiles[head], head, block)
            row_max = jnp.max(scores, axis=-1, keepdims=True)
            exponent = jnp.exp(scores - row_max)
            row_total = jnp.sum(exponent, axis=-1, keepdims=True)
            weights = (exponent * (1.0 / row_total)).astype(BF16)
            part = dot(weights, head_values[head])
            mixed = part if mixed is None else mixed + part
            totals = jnp.where(lane == head, row_max + jnp.log(row_total), totals)
        mixed_ref[rows, :] = mixed.astype(BF16)
        total_ref[rows, :] = totals


class Input:
    def __init__(self, copies, buffer):
        self.copies, self.buffer, self.shape = copies, buffer, buffer.shape
        for copy in copies:
            copy.start()

    def __getitem__(self, index):
        for copy in self.copies:
            copy.wait()
        self.copies = ()
        return self.buffer[index]


class Output:
    def __init__(self, copy, buffer):
        self.copy, self.buffer, self.shape, self.left = copy, buffer, buffer.shape, False

    def __getitem__(self, index):
        return self.buffer[index]

    def __setitem__(self, index, values):
        self.buffer[index] = values

    def leave(self):
        if not self.left:
            self.copy.start()
        self.left = True


def call(kernel, name, outs, smem, operands, scratch=(), limit=60, flops=10**5, moved=10**4):
    groups = [entry if isinstance(entry, tuple) else (entry,) for entry in operands]
    arrays = [array for group in groups for array in group]
    anywhere = pl.BlockSpec(memory_space=pl.ANY)
    held = [
        pltpu.VMEM((len(group),) * (len(group) > 1) + group[0].shape, group[0].dtype) for group in groups
    ] + [pltpu.VMEM(shape, kind) for shape, kind in outs]

    def body(*refs):
        refs = list(refs)

        def take(count):
            taken = refs[:count]
            del refs[:count]
            return taken

        scalars, sources, targets = take(len(smem)), take(len(arrays)), take(len(outs))
        in_buffers, out_buffers = take(len(groups)), take(len(outs))
        in_sems, out_sems = take(2)
        inputs, number = [], 0
        for group, buffer in zip(groups, in_buffers):
            copies = []
            for m in range(len(group)):
                place = buffer if len(group) == 1 else buffer.at[scalars[0][0, 0] ^ m]
                copies.append(pltpu.make_async_copy(sources[number], place, in_sems.at[number]))
                number += 1
            inputs.append(Input(copies, buffer))
        outputs = [
            Output(pltpu.make_async_copy(buffer, target, out_sems.at[i]), buffer)
            for i, (buffer, target) in enumerate(zip(out_buffers, targets))
        ]
        kernel(*scalars, *inputs, *outputs, *refs)
        for entry in inputs:
            for copy in entry.copies:
                copy.wait()
        for entry in outputs:
            entry.leave()
        for entry in outputs:
            entry.copy.wait()

    return pl.pallas_call(
        body,
        out_shape=tuple(jax.ShapeDtypeStruct(shape, kind) for shape, kind in outs),
        in_specs=[pl.BlockSpec(memory_space=pltpu.SMEM)] * len(smem) + [anywhere] * len(arrays),
        out_specs=(anywhere,) * len(outs),
        scratch_shapes=held
        + [pltpu.SemaphoreType.DMA((len(arrays),)), pltpu.SemaphoreType.DMA((len(outs),))]
        + [pltpu.VMEM(shape, kind) for shape, kind in scratch],
        compiler_params=pltpu.CompilerParams(vmem_limit_bytes=limit * MIB),
        cost_estimate=pl.CostEstimate(flops=flops, bytes_accessed=moved, transcendentals=0),
        name=name,
    )(*smem, *arrays)


def attend(tokens, gains, weights, table, heads):
    rows, columns = tokens.shape[0], weights[0].shape[0]
    small = ((rows, columns), BF16)
    return call(
        functools.partial(attend_kernel, heads, columns // heads),
        "attend",
        ((tokens.shape, BF16), small, small, small, small, ((rows, TILE), F32)),
        (table,),
        (tokens, gains, *weights),
    )


def hidden_kernel(tensor_ref, place_ref, tokens_ref, mixed_ref, weight_ref, gain_ref, router_ref, routes_ref, cot_ref, hidden_ref, own_ref, gate_ref, both):
    width = tokens_ref.shape[1]
    experts = router_ref.shape[0]
    gain = gain_ref[1:2, :]
    for block in range(tokens_ref.shape[0] // TILE):
        rows = pl.ds(block * TILE, TILE)
        hidden = tokens_ref[rows, :].astype(F32)
        for m in range(TENSOR):
            hidden = hidden + dot(mixed_ref[m, rows, :], weight_ref[m])
        hidden_ref[rows, :] = hidden
        normed = (hidden * inv_rms_of(hidden) * gain).astype(BF16)
        probs = softmax(dot_t(normed, router_ref[...]))
        lane = lax.broadcasted_iota(jnp.int32, (TILE, experts), 1)
        gate = jnp.sum(jnp.where(lane == routes_ref[rows, :], probs, 0.0), axis=-1, keepdims=True)
        gate_ref[rows, :] = jnp.broadcast_to(gate, (TILE, TILE))
        both[rows, :width] = normed
        both[rows, width:] = (cot_ref[rows, :].astype(F32) * gate).astype(BF16)
    hidden_ref.leave()
    gate_ref.leave()
    slots = own_ref.shape[0]
    row = lax.broadcasted_iota(jnp.int32, (slots, place_ref.shape[1]), 0)
    own_ref[...] = dot((row == place_ref[...]).astype(BF16), both[...]).astype(BF16)


def softmax(values):
    exponent = jnp.exp(values - jnp.max(values, axis=-1, keepdims=True))
    return exponent / jnp.sum(exponent, axis=-1, keepdims=True)


def expert_kernel(me_ref, f_a, b_a, f_b, b_b, in_ref, out_ref, router_ref, keep_ref, send_ref, active_ref, pre_ref, grad_ref):
    rows = f_a.shape[0]
    experts = router_ref.shape[0]
    lane = lax.broadcasted_iota(jnp.int32, (rows, experts), 1)
    own_hot = (lane == me_ref[0, 0]).astype(F32)
    total = None
    for place, (forward, backward) in enumerate(((f_b, b_b), (f_a, b_a))):
        pre = dot(forward[...], in_ref[...])
        square = pre * pre
        bent = jnp.tanh(GELU_SCALE * (pre + GELU_CUBE * square * pre))
        active = (0.5 * pre * (1.0 + bent)).astype(BF16)
        slope = 0.5 * (1.0 + bent) + 0.5 * pre * (1.0 - bent * bent) * (
            GELU_SCALE * (1.0 + 3.0 * GELU_CUBE * square)
        )
        grad_active = dot_t(backward[...], out_ref[...])
        grad_pre = (grad_active * slope).astype(BF16)
        gate_grad = jnp.sum(active.astype(F32) * grad_active, axis=1, keepdims=True)
        probs = softmax(dot_t(forward[...], router_ref[...]))
        grad_logits = (gate_grad * (own_hot - probs)).astype(BF16)
        back = dot_t(grad_pre, in_ref[...]) + dot(grad_logits, router_ref[...])
        where = pl.ds((1 - place) * rows, rows)
        active_ref[where, :] = active
        pre_ref[where, :] = grad_pre
        if place == 0:
            send_ref[...] = back.astype(BF16)
            send_ref.leave()
        else:
            keep_ref[...] = back
        part = t_dot(grad_logits, forward[...])
        total = part if total is None else total + part
    grad_ref[...] = total


def expert_pair(me, first, second, weight_in, weight_out, router):
    rows, width = first[0].shape
    hidden = weight_in.shape[1]
    return call(
        expert_kernel,
        "expert_pair",
        (
            ((rows, width), F32), ((rows, width), BF16), ((2 * rows, hidden), BF16), ((2 * rows, hidden), BF16),
            (router.shape, F32),
        ),
        (me,),
        (*first, *second, weight_in, weight_out, router),

    )


def result_kernel(active_a, active_b, out_ref, keep_ref, send_ref):
    rows = active_a.shape[0] // 2
    for place, active in enumerate((active_a, active_b)):
        where = pl.ds(place * rows, rows)
        keep_ref[where, :] = dot(active[pl.ds(0, rows), :], out_ref[...])
        send_ref[where, :] = dot(active[pl.ds(rows, rows), :], out_ref[...]).astype(BF16)


def expert_grad_kernel(f0, f1, f2, f3, b0, b1, b2, b3, active_a, active_b, pre_a, pre_b, in_ref, out_ref):
    rows = f0.shape[0]
    forward = jnp.concatenate([f0[...], f1[...], f2[...], f3[...]], axis=0)
    pre = jnp.concatenate([pre_a[...], pre_b[...]], axis=0)
    in_ref[...] = t_dot(forward, pre)
    backward = jnp.concatenate([b0[...], b1[...], b2[...], b3[...]], axis=0)
    active = jnp.concatenate([active_a[...], active_b[...]], axis=0)
    out_ref[...] = t_dot(active, backward)


def back_kernel(
    heads, size, table_ref, core_ref, place_ref, r0, r1, r2, r3, hidden_ref, cot_ref, gain_ref, wo_ref, mixed_ref,
    normed_ref, q_ref, k_ref, v_ref, total_ref, wq_ref, wk_ref, wv_ref, router_a, router_b,
    grad_ref, sums_ref, keep_ref, send_ref, small_ref, gm_ref, attn_ref, qb_ref, kacc, vacc, part_ref,
):
    tok_rows, width = hidden_ref.shape
    columns = q_ref.shape[1]
    chunk = r0.shape[0]
    gain = gain_ref[1:2, :]
    count = LEN // TILE
    norm_part = None
    for block in range(count):
        rows = pl.ds(block * TILE, TILE)
        place = place_ref[rows, :]
        back = None
        for m, returned in enumerate((r0, r1, r2, r3)):
            lane = lax.broadcasted_iota(jnp.int32, (TILE, chunk), 1) + m * chunk
            found = dot((lane == place).astype(BF16), returned[...])
            back = found if back is None else back + found
        hidden = hidden_ref[rows, :]
        inv = inv_rms_of(hidden)
        summed = jnp.sum((back * hidden * inv).reshape(TILE // 8, 8, width), axis=0)
        norm_part = summed if norm_part is None else norm_part + summed
        grad = cot_ref[rows, :].astype(F32) + rms_norm_back(hidden, inv, gain, back)
        grad_ref[rows, :] = grad
        low = grad.astype(BF16)
        attn_ref[rows, :] = low
        gm_ref[rows, :] = dot_t(low, wo_ref[...]).astype(BF16)
    grad_ref.leave()
    keys, all_values = k_ref[...], v_ref[...]
    kacc[...] = jnp.zeros_like(kacc)
    vacc[...] = jnp.zeros_like(vacc)
    all_tiles = [bias_tiles(table_ref, head) for head in range(heads)]
    head_keys = [head_columns(keys, head, size) for head in range(heads)]
    near = [[None] * 3 for _ in range(heads)]
    far = [[None] * 2 for _ in range(heads)]
    for block in range(count):
        rows = pl.ds(block * TILE, TILE)
        queries, grads, totals = q_ref[rows, :], gm_ref[rows, :], total_ref[rows, :]
        query_back = None
        for head in range(heads):
            head_queries = head_columns(queries, head, size)
            head_grads = head_columns(grads, head, size)
            scores = dot_t(head_queries, keys)
            scores = scores + bias_rows(table_ref, all_tiles[head], head, block)
            probs = jnp.exp(scores - totals[:, head : head + 1])
            probs_grad = dot_t(head_grads, all_values)
            inner = jnp.sum(probs_grad * probs, axis=-1, keepdims=True)
            score_grad = (probs * (probs_grad - inner)).astype(BF16)
            part = dot(score_grad, head_keys[head])
            query_back = part if query_back is None else query_back + part
            kacc[...] += t_dot(score_grad, head_queries)
            vacc[...] += t_dot(probs.astype(BF16), head_grads)
            wide = score_grad.astype(F32)
            for other in range(count):
                offset = other - block
                tile = wide[:, other * TILE : (other + 1) * TILE]
                if abs(offset) <= 1:
                    held = near[head][offset + 1]
                    near[head][offset + 1] = tile if held is None else held + tile
                else:
                    side = 0 if offset < 0 else 1
                    summed = jnp.sum(tile.reshape(TILE // 8, 8, TILE), axis=0)
                    held = far[head][side]
                    far[head][side] = summed if held is None else held + summed
        qb_ref[rows, :] = query_back.astype(BF16)
    key_back, value_back = kacc[...].astype(BF16), vacc[...].astype(BF16)
    query_back = qb_ref[...]
    part_ref[...] = dot(query_back, wq_ref[...]) + dot(key_back, wk_ref[...]) + dot(value_back, wv_ref[...])
    half = tok_rows // 2
    extra = keep_ref.shape[0] - half
    core = core_ref[0, 0]
    keep_ref[pl.ds(0, half), :] = part_ref[pl.ds(pl.multiple_of(core * half, half), half), :]
    send_ref[pl.ds(0, half), :] = part_ref[pl.ds(pl.multiple_of((1 - core) * half, half), half), :].astype(BF16)
    router = (router_a[...] + router_b[...]).astype(BF16).astype(F32)
    if extra > router.shape[0]:
        router = jnp.concatenate([router, jnp.zeros((extra - router.shape[0], width), F32)], axis=0)
    keep_ref[pl.ds(half, extra), :] = router
    send_ref[pl.ds(half, extra), :] = router.astype(BF16)
    send_ref.leave()
    keep_ref.leave()
    empty = jnp.zeros((tok_rows, columns), BF16)
    sums_ref[:, : 2 * columns] = t_dot(
        normed_ref[...], jnp.concatenate([query_back, key_back], axis=1)
    ).astype(BF16)
    sums_ref[:, 2 * columns :] = (
        t_dot(normed_ref[...], jnp.concatenate([value_back, empty], axis=1))
        + t_dot(attn_ref[...], jnp.concatenate([empty, mixed_ref[...]], axis=1))
    ).astype(BF16)
    sums_ref.leave()
    bias = bias_sums(heads, near, far)
    bias_row = lax.dot_general(
        jnp.ones((8, TILE), F32), bias, (((1,), (1,)), ((), ())),
        precision=lax.Precision.HIGHEST, preferred_element_type=F32,
    )
    bias_row = jnp.concatenate([bias_row, jnp.zeros((8, width - heads * BUCKETS), F32)], axis=1)
    norm_row = jnp.broadcast_to(jnp.sum(norm_part, axis=0, keepdims=True), (8, width))
    line = lax.broadcasted_iota(jnp.int32, (8, width), 0)
    small_ref[...] = jnp.where(line == 0, norm_row, jnp.where(line == 1, bias_row, 0.0))


def bias_sums(heads, near, far):
    row = lax.broadcasted_iota(jnp.int32, (TILE, TILE), 0)
    col = lax.broadcasted_iota(jnp.int32, (TILE, TILE), 1)

    def fold(values):
        return jnp.sum(values.reshape(TILE // 8, 8, TILE), axis=0)

    edges = tuple(range(8)) + (8,) + THRESHOLDS + (1 << 20,)
    pieces = []
    for head in range(heads):
        for sign in (0, 1):
            for n in range(16):
                piece = jnp.zeros((8, TILE), F32)
                for offset in ((-1, 0) if sign == 0 else (0, 1)):
                    low = 0 if offset == 0 else 1
                    if edges[n + 1] <= low or edges[n] > (TILE - 1 if offset == 0 else 2 * TILE - 1):
                        continue
                    shift = col - row + offset * TILE
                    distance = jnp.abs(shift)
                    inside = (distance >= edges[n]) & (distance < edges[n + 1])
                    if offset == 0:
                        inside = inside & ((shift > 0) if sign else (shift <= 0))
                    piece = piece + fold(jnp.where(inside, near[head][offset + 1], 0.0))
                if n == 15:
                    piece = piece + far[head][sign]
                pieces.append(jnp.sum(piece, axis=0, keepdims=True))
    return jnp.concatenate(pieces, axis=0)


def swap(values, axis, mask):
    size = lax.axis_size(axis)
    return lax.ppermute(values, axis, [(i, i ^ mask) for i in range(size)])


def gather_tensor(values):
    far = swap(values, "tensor", 2)
    near = swap(values, "tensor", 1)
    return values, near, far, swap(far, "tensor", 1)


def exchange_expert(blocks):
    return lax.all_to_all(blocks, "expert", split_axis=0, concat_axis=0, tiled=True)


def after(values, done):
    return lax.optimization_barrier((values, done))[0]


def sum_expert(values, done):
    mask = 1
    while mask < lax.axis_size("expert"):
        if 2 * mask >= lax.axis_size("expert"):
            values = after(values, done)
        values = values + swap(values, "expert", mask)
        mask = 2 * mask
    return values


def on_device(
    tokens,
    norm_first,
    w_query,
    w_key,
    w_value,
    w_output,
    bias_table,
    norm_second,
    w_router,
    w_expert_in,
    w_expert_out,
    routes,
    cotangent,
):
    tok_rows, width = tokens.shape
    experts = w_router.shape[1]
    capacity = max(2, 3 * tok_rows // (2 * experts))
    quarter = -(-capacity // TENSOR)
    heads_here = bias_table.shape[1]
    columns = w_query.shape[1]
    chunk_rows = experts * quarter
    half = tok_rows // 2
    extra = max(16, experts)
    my_tensor = lax.axis_index("tensor")
    my_expert = lax.axis_index("expert").astype(jnp.int32).reshape(1, 1)
    core = (my_tensor & 1).astype(jnp.int32)
    weight_in = w_expert_in[0]
    weight_out = w_expert_out[0]
    router = w_router.T
    weights = (w_query.T, w_key.T, w_value.T)
    table = bias_table.T.astype(F32)
    gains = jnp.stack([norm_first, norm_second]).astype(F32)

    normed, queries, keys, values, mixed, totals = attend(tokens, gains, weights, table, heads_here)

    chosen = routes[:, 0]
    route_hot = chosen[:, None] == jnp.arange(experts, dtype=jnp.int32)[None, :]
    places = jnp.arange(tok_rows, dtype=jnp.int32)
    before = (places[:, None] > places[None, :]).astype(BF16)
    earlier = dot(before, route_hot.astype(BF16))
    slot_index = jnp.sum(jnp.where(route_hot, earlier, 0.0), axis=1).astype(jnp.int32)
    chunk = (slot_index // quarter) ^ my_tensor
    place = (chunk * experts + chosen) * quarter + slot_index % quarter

    output_parts = gather_tensor(w_output)
    hidden, own, gate = call(
        hidden_kernel,
        "hidden",
        (((tok_rows, width), F32), ((chunk_rows, 2 * width), BF16), ((tok_rows, TILE), F32)),
        (my_tensor.astype(jnp.int32).reshape(1, 1),),
        (
            place[None, :], tokens, gather_tensor(after(mixed, output_parts[2])), output_parts, gains, router,
            routes, cotangent,
        ),
        scratch=(((tok_rows, 2 * width), BF16),),
    )
    arrived = exchange_expert(own.reshape(experts, quarter, 2 * width)).reshape(chunk_rows, 2 * width)
    forward, backward = arrived[:, :width], arrived[:, width:]
    forward_far, backward_far = swap(forward, "tensor", 2), swap(backward, "tensor", 2)
    forward_near, backward_near = swap(forward, "tensor", 1), swap(backward, "tensor", 1)

    keep_a, send_a, active_a, pre_a, router_a = expert_pair(
        my_expert, (forward, backward), (forward_near, backward_near), weight_in, weight_out, router
    )
    forward_diag = swap(after(forward_far, active_a), "tensor", 1)
    backward_diag = swap(after(backward_far, active_a), "tensor", 1)
    got_a = swap(send_a, "tensor", 1)
    keep_b, send_b, active_b, pre_b, router_b = expert_pair(
        my_expert, (forward_far, backward_far), (forward_diag, backward_diag), weight_in, weight_out, router
    )
    other = (keep_b + swap(send_b, "tensor", 1).astype(F32)).astype(BF16)
    other_back = swap(other, "tensor", 2)

    keep_r, send_r = call(
        result_kernel,
        "expert_result",
        (((2 * chunk_rows, width), F32), ((2 * chunk_rows, width), BF16)),
        (),
        (after(active_a, other), active_b, weight_out),
    )
    own_back = ((keep_a + got_a.astype(F32)) + other_back.astype(F32)).astype(BF16)
    own_back = after(own_back, send_r)
    home = exchange_expert(own_back.reshape(experts, quarter, width)).reshape(chunk_rows, width)
    got_r = swap(send_r, "tensor", 1).astype(F32)
    far_result = swap((keep_r[chunk_rows:] + got_r[chunk_rows:]).astype(BF16), "tensor", 2)
    grad_expert_in, grad_expert_out = call(
        expert_grad_kernel,
        "expert_grads",
        ((weight_in.shape, F32), (weight_out.shape, F32)),
        (),
        (
            forward, forward_near, forward_far, forward_diag, backward, backward_near, backward_far, backward_diag,
            after(active_a, got_r), active_b, pre_a, pre_b,
        ),
    )
    own_result = ((keep_r[:chunk_rows] + got_r[:chunk_rows]) + far_result.astype(F32)).astype(BF16)
    home = after(home, (own_result, grad_expert_in))
    result = exchange_expert(after(own_result, home).reshape(experts, quarter, width)).reshape(chunk_rows, width)
    home_far = swap(home, "tensor", 2)
    returned_back = (home, swap(home, "tensor", 1), home_far, after(swap(home_far, "tensor", 1), result))

    small = ((8, width), F32)
    grad_hidden, sums, keep, send, small = call(
        functools.partial(back_kernel, heads_here, columns // heads_here),
        "layer_back",
        (
            ((tok_rows, width), F32), ((width, 4 * columns), BF16), ((half + extra, width), F32),
            ((half + extra, width), BF16), ((8, width), F32),
        ),
        (table, core.reshape(1, 1)),
        (
            place[:, None], *returned_back, hidden, cotangent, gains, w_output, mixed, normed,
            queries, keys, values, totals, *weights, router_a, router_b,
        ),
        scratch=(
            ((tok_rows, columns), BF16), ((tok_rows, width), BF16), ((tok_rows, columns), BF16),
            ((tok_rows, columns), F32), ((tok_rows, columns), F32), ((tok_rows, width), F32),
        ),
    )

    pair = (keep + swap(send, "tensor", 1).astype(F32)).astype(BF16)
    total = (pair.astype(F32) + swap(pair, "tensor", 2).astype(F32)).astype(BF16)
    near = swap(total[:half], "tensor", 1)
    low = jnp.where(core == 1, near, total[:half]).astype(F32)
    high = jnp.where(core == 1, total[:half], near).astype(F32)
    normed_back = jnp.concatenate([low, high])
    inputs = tokens.astype(F32)
    inv_first = inv_rms_of(inputs)
    gain_first = gains[0:1]
    norm_first_part = jnp.sum(normed_back * inputs * inv_first, axis=0, keepdims=True)
    grad_tokens = grad_hidden + rms_norm_back(inputs, inv_first, gain_first, normed_back)

    returned = gather_tensor(after(result, total))
    place_hot = (
        place[:, None] == jnp.arange(TENSOR * chunk_rows, dtype=jnp.int32)[None, :]
    ).astype(BF16)
    layer_out = (hidden + gate[:, :1] * dot(place_hot, jnp.concatenate(returned))).astype(BF16)

    grads = exchange_expert(sums.reshape(lax.axis_size("expert"), -1, 4 * columns))
    grads = jnp.sum(grads.astype(F32), axis=0)
    small = sum_expert(jnp.concatenate([total[half : half + experts].astype(F32), norm_first_part, small[:2]]), grads)
    bias_size = BUCKETS * heads_here
    return (
        layer_out,
        grad_tokens,
        small[experts],
        grads[:, :columns],
        grads[:, columns : 2 * columns],
        grads[:, 2 * columns : 3 * columns],
        grads[:, 3 * columns :].T,
        small[experts + 2, :bias_size].reshape(heads_here, BUCKETS).T,
        small[experts + 1],
        small[:experts].T,
        grad_expert_in[None],
        grad_expert_out[None],
    )


def solution(mesh):
    return jax.shard_map(
        on_device,
        mesh=mesh,
        in_specs=(
            P("expert", None),
            P(),
            P(None, "tensor"),
            P(None, "tensor"),
            P(None, "tensor"),
            P("tensor", None),
            P(None, "tensor"),
            P(),
            P(),
            P("expert", None, "tensor"),
            P("expert", "tensor", None),
            P("expert", None),
            P("expert", None),
        ),
        out_specs=(
            P("expert", None),
            P("expert", None),
            P(),
            P("expert", "tensor"),
            P("expert", "tensor"),
            P("expert", "tensor"),
            P("tensor", "expert"),
            P(None, "tensor"),
            P(),
            P(),
            P("expert", None, "tensor"),
            P("expert", "tensor", None),
        ),
        check_vma=False,
    )
```

```python
import functools

import jax
import jax.numpy as jnp
from jax import lax
from jax.experimental import pallas as pl
from jax.experimental.pallas import tpu as pltpu
from jax.sharding import PartitionSpec as P

BUCKETS = 32
LEN = 512
TENSOR = 4
PAIRED = 8

EPSILON = 1e-06
THRESHOLDS = (12, 16, 23, 32, 46, 64, 91)
BF16 = jnp.bfloat16
F32 = jnp.float32
GELU_SCALE = (2.0 / 3.141592653589793) ** 0.5
GELU_CUBE = 0.044715
MIB = 1024 * 1024


def dot(left, right):
    return jnp.dot(left, right, preferred_element_type=F32)


def dot_t(left, right):
    return lax.dot_general(left, right, (((1,), (1,)), ((), ())), preferred_element_type=F32)


def t_dot(left, right):
    return lax.dot_general(left, right, (((0,), (0,)), ((), ())), preferred_element_type=F32)


def inv_rms_of(values):
    return lax.rsqrt(jnp.mean(values * values, axis=-1, keepdims=True) + EPSILON)


def rms_norm_back(values, inv_rms, gain, grad):
    scaled = gain * grad
    inner = jnp.mean(scaled * values, axis=-1, keepdims=True)
    return inv_rms * scaled - values * (inv_rms * inv_rms * inv_rms * inner)


TILE = 128


def skew(tile):
    return pltpu.roll(tile, 0, 1, stride=1, stride_axis=0)


def diagonal_sums(tile):
    row = lax.broadcasted_iota(jnp.int32, (TILE, TILE), 0)
    turn = (row + lax.broadcasted_iota(jnp.int32, (TILE, TILE), 1) == TILE - 1).astype(F32)
    turned = lax.dot_general(
        turn, tile, (((1,), (0,)), ((), ())), precision=lax.Precision.HIGHEST, preferred_element_type=F32
    )
    return jnp.sum(pltpu.roll(turned, 1, 1, stride=1, stride_axis=0), axis=0, keepdims=True)


def bias_tiles(table_ref, head):
    lane = lax.broadcasted_iota(jnp.int32, (8, TILE), 1)
    place = lax.broadcasted_iota(jnp.int32, (TILE, TILE), 1)

    def chain(base, distance):
        line = jnp.full((8, TILE), table_ref[head, base], F32)
        for n in range(1, 8):
            line = jnp.where(distance >= n, table_ref[head, base + n], line)
        for n, threshold in enumerate((8,) + THRESHOLDS):
            line = jnp.where(distance >= threshold, table_ref[head, base + 8 + n], line)
        return jnp.broadcast_to(line[0:1, :], (TILE, TILE))

    ahead = skew(jnp.where(place == 0, table_ref[head, 0], chain(16, lane)))
    behind = skew(chain(0, TILE - lane))
    upper = place >= lax.broadcasted_iota(jnp.int32, (TILE, TILE), 0)
    return [
        jnp.where(upper, behind, table_ref[head, 15]),
        jnp.where(upper, ahead, behind),
        jnp.where(upper, table_ref[head, 31], ahead),
    ]


def bias_rows(table_ref, tiles, head, block):
    parts = []
    for other in range(LEN // TILE):
        offset = other - block
        if offset < -1:
            parts.append(jnp.full((TILE, TILE), table_ref[head, 15], F32))
        elif offset > 1:
            parts.append(jnp.full((TILE, TILE), table_ref[head, 31], F32))
        else:
            parts.append(tiles[offset + 1])
    return jnp.concatenate(parts, axis=1)


def head_columns(values, head, size):
    lane = lax.broadcasted_iota(jnp.int32, values.shape, 1)
    return jnp.where((lane >= head * size) & (lane < (head + 1) * size), values, jnp.zeros_like(values))


def attend_kernel(heads, size, table_ref, tokens_ref, gain_ref, wq_ref, wk_ref, wv_ref, q_ref, k_ref, v_ref, mixed_ref, total_ref):
    values = tokens_ref[...].astype(F32)
    normed = (values * inv_rms_of(values) * gain_ref[...].astype(F32).reshape(1, -1)).astype(BF16)
    q_ref[...] = dot_t(normed, wq_ref[...]).astype(BF16)
    q_ref.leave()
    k_ref[...] = dot_t(normed, wk_ref[...]).astype(BF16)
    k_ref.leave()
    v_ref[...] = dot_t(normed, wv_ref[...]).astype(BF16)
    v_ref.leave()
    all_tiles = [bias_tiles(table_ref, head) for head in range(heads)]
    keys = k_ref[...]
    head_values = [head_columns(v_ref[...], head, size) for head in range(heads)]
    for block in range(LEN // TILE):
        rows = pl.ds(block * TILE, TILE)
        queries = q_ref[rows, :]
        mixed = None
        lane = lax.broadcasted_iota(jnp.int32, (TILE, TILE), 1)
        totals = jnp.zeros((TILE, TILE), F32)
        for head in range(heads):
            scores = dot_t(head_columns(queries, head, size), keys)
            scores = scores + bias_rows(table_ref, all_tiles[head], head, block)
            row_max = jnp.max(scores, axis=-1, keepdims=True)
            exponent = jnp.exp(scores - row_max)
            row_total = jnp.sum(exponent, axis=-1, keepdims=True)
            weights = (exponent * (1.0 / row_total)).astype(BF16)
            part = dot(weights, head_values[head])
            mixed = part if mixed is None else mixed + part
            totals = jnp.where(lane == head, row_max + jnp.log(row_total), totals)
        mixed_ref[rows, :] = mixed.astype(BF16)
        total_ref[rows, :] = totals


class Input:
    def __init__(self, copies, buffer):
        self.copies, self.buffer, self.shape = copies, buffer, buffer.shape
        for copy in copies:
            copy.start()

    def __getitem__(self, index):
        for copy in self.copies:
            copy.wait()
        self.copies = ()
        return self.buffer[index]


class Output:
    def __init__(self, copy, buffer):
        self.copy, self.buffer, self.shape, self.left = copy, buffer, buffer.shape, False

    def __getitem__(self, index):
        return self.buffer[index]

    def __setitem__(self, index, values):
        self.buffer[index] = values

    def leave(self):
        if not self.left:
            self.copy.start()
        self.left = True


def call(kernel, name, outs, smem, operands, scratch=(), limit=60, flops=10**5, moved=10**4):
    groups = [entry if isinstance(entry, tuple) else (entry,) for entry in operands]
    arrays = [array for group in groups for array in group]
    anywhere = pl.BlockSpec(memory_space=pl.ANY)
    held = [
        pltpu.VMEM((len(group),) * (len(group) > 1) + group[0].shape, group[0].dtype) for group in groups
    ] + [pltpu.VMEM(shape, kind) for shape, kind in outs]

    def body(*refs):
        refs = list(refs)

        def take(count):
            taken = refs[:count]
            del refs[:count]
            return taken

        scalars, sources, targets = take(len(smem)), take(len(arrays)), take(len(outs))
        in_buffers, out_buffers = take(len(groups)), take(len(outs))
        in_sems, out_sems = take(2)
        inputs, number = [], 0
        for group, buffer in zip(groups, in_buffers):
            copies = []
            for m in range(len(group)):
                place = buffer if len(group) == 1 else buffer.at[scalars[0][0, 0] ^ m]
                copies.append(pltpu.make_async_copy(sources[number], place, in_sems.at[number]))
                number += 1
            inputs.append(Input(copies, buffer))
        outputs = [
            Output(pltpu.make_async_copy(buffer, target, out_sems.at[i]), buffer)
            for i, (buffer, target) in enumerate(zip(out_buffers, targets))
        ]
        kernel(*scalars, *inputs, *outputs, *refs)
        for entry in inputs:
            for copy in entry.copies:
                copy.wait()
        for entry in outputs:
            entry.leave()
        for entry in outputs:
            entry.copy.wait()

    return pl.pallas_call(
        body,
        out_shape=tuple(jax.ShapeDtypeStruct(shape, kind) for shape, kind in outs),
        in_specs=[pl.BlockSpec(memory_space=pltpu.SMEM)] * len(smem) + [anywhere] * len(arrays),
        out_specs=(anywhere,) * len(outs),
        scratch_shapes=held
        + [pltpu.SemaphoreType.DMA((len(arrays),)), pltpu.SemaphoreType.DMA((len(outs),))]
        + [pltpu.VMEM(shape, kind) for shape, kind in scratch],
        compiler_params=pltpu.CompilerParams(vmem_limit_bytes=limit * MIB),
        cost_estimate=pl.CostEstimate(flops=flops, bytes_accessed=moved, transcendentals=0),
        name=name,
    )(*smem, *arrays)


def attend(tokens, gains, weights, table, heads):
    rows, columns = tokens.shape[0], weights[0].shape[0]
    small = ((rows, columns), BF16)
    return call(
        functools.partial(attend_kernel, heads, columns // heads),
        "attend",
        (small, small, small, small, ((rows, TILE), F32)),
        (table,),
        (tokens, gains, *weights),
    )


def hidden_kernel(tensor_ref, place_ref, tokens_ref, mixed_ref, weight_ref, gain_ref, router_ref, routes_ref, cot_ref, hidden_ref, own_ref, gate_ref, both):
    width = tokens_ref.shape[1]
    experts = router_ref.shape[0]
    gain = gain_ref[...].astype(F32).reshape(1, -1)
    for block in range(tokens_ref.shape[0] // TILE):
        rows = pl.ds(block * TILE, TILE)
        hidden = tokens_ref[rows, :].astype(F32)
        for m in range(TENSOR):
            hidden = hidden + dot(mixed_ref[m, rows, :], weight_ref[m])
        hidden_ref[rows, :] = hidden
        normed = (hidden * inv_rms_of(hidden) * gain).astype(BF16)
        probs = softmax(dot_t(normed, router_ref[...]))
        lane = lax.broadcasted_iota(jnp.int32, (TILE, experts), 1)
        gate = jnp.sum(jnp.where(lane == routes_ref[rows, :], probs, 0.0), axis=-1, keepdims=True)
        gate_ref[rows, :] = jnp.broadcast_to(gate, (TILE, TILE))
        both[rows, :width] = normed
        both[rows, width:] = (cot_ref[rows, :].astype(F32) * gate).astype(BF16)
    hidden_ref.leave()
    gate_ref.leave()
    slots = own_ref.shape[0]
    row = lax.broadcasted_iota(jnp.int32, (slots, place_ref.shape[1]), 0)
    own_ref[...] = dot((row == place_ref[...]).astype(BF16), both[...]).astype(BF16)


def softmax(values):
    exponent = jnp.exp(values - jnp.max(values, axis=-1, keepdims=True))
    return exponent / jnp.sum(exponent, axis=-1, keepdims=True)


def expert_kernel(me_ref, f_b, in_ref, b_b, out_ref, router_ref, f_a, b_a, keep_ref, send_ref, keep_r_ref, send_r_ref, active_ref, pre_ref, grad_ref):
    rows = f_a.shape[0]
    experts = router_ref.shape[0]
    lane = lax.broadcasted_iota(jnp.int32, (rows, experts), 1)
    own_hot = (lane == me_ref[0, 0]).astype(F32)
    total = None
    for place, (forward, backward) in enumerate(((f_b, b_b), (f_a, b_a))):
        pre = dot(forward[...], in_ref[...])
        square = pre * pre
        bent = jnp.tanh(GELU_SCALE * (pre + GELU_CUBE * square * pre))
        active = (0.5 * pre * (1.0 + bent)).astype(BF16)
        slope = 0.5 * (1.0 + bent) + 0.5 * pre * (1.0 - bent * bent) * (
            GELU_SCALE * (1.0 + 3.0 * GELU_CUBE * square)
        )
        grad_active = dot_t(backward[...], out_ref[...])
        grad_pre = (grad_active * slope).astype(BF16)
        gate_grad = jnp.sum(active.astype(F32) * grad_active, axis=1, keepdims=True)
        probs = softmax(dot_t(forward[...], router_ref[...]))
        grad_logits = (gate_grad * (own_hot - probs)).astype(BF16)
        back = dot_t(grad_pre, in_ref[...]) + dot(grad_logits, router_ref[...])
        where = pl.ds((1 - place) * rows, rows)
        active_ref[where, :] = active
        pre_ref[where, :] = grad_pre
        if place == 0:
            send_ref[...] = back.astype(BF16)
            send_ref.leave()
            send_r_ref[...] = dot(active, out_ref[...]).astype(BF16)
            send_r_ref.leave()
        else:
            keep_ref[...] = back
            keep_ref.leave()
            keep_r_ref[...] = dot(active, out_ref[...])
        part = t_dot(grad_logits, forward[...])
        total = part if total is None else total + part
    grad_ref[...] = total


def expert_pair(me, first, second, weight_in, weight_out, router):
    rows, width = first[0].shape
    hidden = weight_in.shape[1]
    return call(
        expert_kernel,
        "expert_pair",
        (
            ((rows, width), F32), ((rows, width), BF16), ((rows, width), F32), ((rows, width), BF16),
            ((2 * rows, hidden), BF16), ((2 * rows, hidden), BF16),
            (router.shape, F32),
        ),
        (me,),
        (second[0], weight_in, second[1], weight_out, router, *first),

    )


def expert_grad_kernel(f0, f1, f2, f3, b0, b1, b2, b3, active_a, active_b, pre_a, pre_b, in_ref, out_ref):
    rows = f0.shape[0]
    forward = jnp.concatenate([f0[...], f1[...], f2[...], f3[...]], axis=0)
    pre = jnp.concatenate([pre_a[...], pre_b[...]], axis=0)
    in_ref[...] = t_dot(forward, pre)
    backward = jnp.concatenate([b0[...], b1[...], b2[...], b3[...]], axis=0)
    active = jnp.concatenate([active_a[...], active_b[...]], axis=0)
    out_ref[...] = t_dot(active, backward)


def packed(rows, count):
    size = rows.shape[0] // count
    return jnp.concatenate([rows[n * size : (n + 1) * size] for n in range(count)], axis=1)


def unpacked(rows, count):
    size = rows.shape[1] // count
    return jnp.concatenate([rows[:, n * size : (n + 1) * size] for n in range(count)], axis=0)


def hidden_back_kernel(
    devices, place_ref, hidden_ref, r0, r1, r2, r3, cot_ref, gain_ref, wo_ref, mixed_ref,
    grad_ref, gm_ref, turned_ref, norm_ref, sums_ref, attn_ref,
):
    tok_rows, width = hidden_ref.shape
    columns = mixed_ref.shape[1]
    chunk = r0.shape[0]
    gain = gain_ref[...].astype(F32).reshape(1, -1)
    norm_part = None
    for block in range(tok_rows // TILE):
        rows = pl.ds(block * TILE, TILE)
        place = place_ref[rows, :]
        back = None
        for m, returned in enumerate((r0, r1, r2, r3)):
            lane = lax.broadcasted_iota(jnp.int32, (TILE, chunk), 1) + m * chunk
            found = dot((lane == place).astype(BF16), returned[...])
            back = found if back is None else back + found
        hidden = hidden_ref[rows, :]
        inv = inv_rms_of(hidden)
        summed = jnp.sum((back * hidden * inv).reshape(TILE // 8, 8, width), axis=0)
        norm_part = summed if norm_part is None else norm_part + summed
        grad = cot_ref[rows, :].astype(F32) + rms_norm_back(hidden, inv, gain, back)
        grad_ref[rows, :] = grad
        low = grad.astype(BF16)
        attn_ref[rows, :] = low
        gm_ref[rows, :] = dot_t(low, wo_ref[...]).astype(BF16)
    grad_ref.leave()
    gm_ref.leave()
    unit = lax.broadcasted_iota(jnp.int32, (columns, columns), 0)
    unit = (unit == lax.broadcasted_iota(jnp.int32, (columns, columns), 1)).astype(BF16)
    sums = dot(dot_t(unit, mixed_ref[...]).astype(BF16), attn_ref[...]).T
    if devices == PAIRED:
        size = width // devices
        sums = jnp.concatenate([packed(sums[n * size : (n + 1) * size], 4) for n in range(devices)], axis=0)
    sums_ref[...] = sums.astype(BF16)
    sums_ref.leave()
    turned_ref[...] = dot_t(wo_ref[...], attn_ref[...]).astype(BF16)
    norm_ref[...] = norm_part


def back_kernel(
    heads, size, devices, table_ref, core_ref, q_ref, k_ref, v_ref, gm_ref, turned_ref, total_ref,
    tokens_ref, gain_ref, wq_ref, wk_ref, wv_ref, router_a, router_b, norm_ref,
    sums_ref, keep_ref, send_ref, small_ref, back_t, turn_t, part_ref, normed_ref, qb_ref,
):
    tok_rows, width = tokens_ref.shape
    columns = q_ref.shape[1]
    count = LEN // TILE
    keys, all_values = k_ref[...], v_ref[...]
    back_t[...] = jnp.zeros_like(back_t)
    inputs = tokens_ref[...].astype(F32)
    inv_first = inv_rms_of(inputs)
    normed_ref[...] = (inputs * inv_first * gain_ref[...].astype(F32).reshape(1, -1)).astype(BF16)
    turn_t[pl.ds(0, columns), :] = dot_t(wq_ref[...], normed_ref[...]).astype(BF16)
    turn_t[pl.ds(columns, columns), :] = turned_ref[...]
    all_tiles = [bias_tiles(table_ref, head) for head in range(heads)]
    head_keys = [head_columns(keys, head, size) for head in range(heads)]
    near = [[None] * 3 for _ in range(heads)]
    far = [[None] * 2 for _ in range(heads)]
    for block in range(count):
        rows = pl.ds(block * TILE, TILE)
        queries, grads, totals = q_ref[rows, :], gm_ref[rows, :], total_ref[rows, :]
        query_back = None
        for head in range(heads):
            head_queries = head_columns(queries, head, size)
            head_grads = head_columns(grads, head, size)
            scores = dot_t(head_queries, keys)
            scores = scores + bias_rows(table_ref, all_tiles[head], head, block)
            probs = jnp.exp(scores - totals[:, head : head + 1])
            probs_grad = dot_t(head_grads, all_values)
            inner = jnp.sum(probs_grad * probs, axis=-1, keepdims=True)
            score_grad = (probs * (probs_grad - inner)).astype(BF16)
            part = dot(score_grad, head_keys[head])
            query_back = part if query_back is None else query_back + part
            mine = pl.ds(head * size, size)
            back_t[mine, :] += dot(turn_t[mine, rows], score_grad)
            mine = pl.ds(columns + head * size, size)
            back_t[mine, :] += dot(turn_t[mine, rows], probs.astype(BF16))
            wide = score_grad.astype(F32)
            for other in range(count):
                offset = other - block
                tile = wide[:, other * TILE : (other + 1) * TILE]
                if abs(offset) <= 1:
                    held = near[head][offset + 1]
                    near[head][offset + 1] = tile if held is None else held + tile
                else:
                    side = 0 if offset < 0 else 1
                    summed = jnp.sum(tile.reshape(TILE // 8, 8, TILE), axis=0)
                    held = far[head][side]
                    far[head][side] = summed if held is None else held + summed
        qb_ref[rows, :] = query_back.astype(BF16)
    query_back = qb_ref[...]
    key_t = back_t[pl.ds(0, columns), :].astype(BF16)
    value_t = back_t[pl.ds(columns, columns), :].astype(BF16)
    part_ref[...] = dot(query_back, wq_ref[...]) + t_dot(key_t, wk_ref[...]) + t_dot(value_t, wv_ref[...])
    half = tok_rows // 2
    core = core_ref[0, 0]
    keep_ref[...] = part_ref[pl.ds(pl.multiple_of(core * half, half), half), :]
    keep_ref.leave()
    send_ref[...] = part_ref[pl.ds(pl.multiple_of((1 - core) * half, half), half), :].astype(BF16)
    send_ref.leave()
    bias_row = jnp.concatenate([bias_sums(heads, near, far), jnp.zeros((8, width - TILE), F32)], axis=1)
    norm_row = jnp.broadcast_to(jnp.sum(norm_ref[...], axis=0, keepdims=True), (8, width))
    first_part = jnp.sum(part_ref[...] * tokens_ref[...].astype(F32) * inv_first, axis=0, keepdims=True)
    line = lax.broadcasted_iota(jnp.int32, (8, width), 0)
    lines = jnp.where(line == 0, first_part, jnp.where(line == 1, norm_row, jnp.where(line == 2, bias_row, 0.0)))
    small = jnp.concatenate([router_a[...] + router_b[...], lines], axis=0)
    small_ref[...] = small
    small_ref.leave()
    unit = lax.broadcasted_iota(jnp.int32, (columns, columns), 0)
    unit = (unit == lax.broadcasted_iota(jnp.int32, (columns, columns), 1)).astype(BF16)
    turned = (dot_t(unit, query_back).astype(BF16), key_t, value_t)
    parts = [dot(rows, normed_ref[...]) for rows in turned]
    sums = jnp.concatenate(parts, axis=0).T
    if devices == PAIRED:
        size = width // devices
        blocks = [sums[n * size : (n + 1) * size] for n in range(devices)]
        sums = jnp.concatenate(
            [
                piece
                for block in blocks
                for piece in (packed(block[:, : 2 * columns], 2), packed(block[:, 2 * columns :], 4), small)
            ],
            axis=0,
        )
    sums_ref[...] = sums.astype(BF16)
    sums_ref.leave()


def bias_sums(heads, near, far):
    upper = lax.broadcasted_iota(jnp.int32, (TILE, TILE), 1) >= lax.broadcasted_iota(jnp.int32, (TILE, TILE), 0)
    edges = tuple(range(8)) + (8,) + THRESHOLDS + (1 << 20,)
    lane = lax.broadcasted_iota(jnp.int32, (TILE, TILE), 0)
    place = lax.broadcasted_iota(jnp.int32, (TILE, TILE), 1)
    total = jnp.zeros((8, TILE), F32)

    def bucket(distance):
        found = jnp.zeros((TILE, TILE), jnp.int32)
        for n in range(1, 16):
            found = jnp.where(distance >= edges[n], n, found)
        return found

    for head in range(heads):
        before, here, beyond = near[head]
        start = head * BUCKETS
        ahead = diagonal_sums(jnp.where(upper, here, beyond))
        behind = diagonal_sums(jnp.where(upper, before, here))
        outside = (
            jnp.sum(jnp.where(upper, 0.0, before), axis=0, keepdims=True) + jnp.sum(far[head][0], axis=0, keepdims=True),
            jnp.sum(jnp.where(upper, beyond, 0.0), axis=0, keepdims=True) + jnp.sum(far[head][1], axis=0, keepdims=True),
        )
        targets = (
            start + jnp.where(lane == 0, 0, 16 + bucket(lane)),
            start + bucket(TILE - lane),
            jnp.full((TILE, TILE), start + 15, jnp.int32),
            jnp.full((TILE, TILE), start + 31, jnp.int32),
        )
        for row, target in zip((ahead, behind, *outside), targets):
            total = total + lax.dot_general(
                jnp.broadcast_to(row, (8, TILE)), (place == target).astype(F32), (((1,), (0,)), ((), ())),
                precision=lax.Precision.HIGHEST, preferred_element_type=F32,
            )
    return total


def swap(values, axis, mask):
    size = lax.axis_size(axis)
    return lax.ppermute(values, axis, [(i, i ^ mask) for i in range(size)])


def gather_tensor(values):
    far = swap(values, "tensor", 2)
    near = swap(values, "tensor", 1)
    return values, near, far, swap(far, "tensor", 1)


def exchange_expert(blocks):
    return lax.all_to_all(blocks, "expert", split_axis=0, concat_axis=0, tiled=True)


def after(values, done):
    return lax.optimization_barrier((values, done))[0]


def sum_expert(values):
    mask = 1
    while mask < lax.axis_size("expert"):
        values = values + swap(values, "expert", mask)
        mask = 2 * mask
    return values


def on_device(
    tokens,
    norm_first,
    w_query,
    w_key,
    w_value,
    w_output,
    bias_table,
    norm_second,
    w_router,
    w_expert_in,
    w_expert_out,
    routes,
    cotangent,
):
    tok_rows, width = tokens.shape
    experts = w_router.shape[1]
    capacity = max(2, 3 * tok_rows // (2 * experts))
    quarter = -(-capacity // TENSOR)
    heads_here = bias_table.shape[1]
    columns = w_query.shape[1]
    chunk_rows = experts * quarter
    half = tok_rows // 2
    devices = lax.axis_size("expert")
    paired = devices == PAIRED
    my_tensor = lax.axis_index("tensor")
    my_expert = lax.axis_index("expert").astype(jnp.int32).reshape(1, 1)
    core = (my_tensor & 1).astype(jnp.int32)
    weight_in = w_expert_in[0]
    weight_out = w_expert_out[0]
    router = w_router.T
    weights = (w_query.T, w_key.T, w_value.T)
    table = bias_table.T.astype(F32)

    queries, keys, values, mixed, totals = attend(tokens, norm_first, weights, table, heads_here)

    chosen = routes[:, 0]
    route_hot = chosen[:, None] == jnp.arange(experts, dtype=jnp.int32)[None, :]
    places = jnp.arange(tok_rows, dtype=jnp.int32)
    before = (places[:, None] > places[None, :]).astype(BF16)
    earlier = dot(before, route_hot.astype(BF16))
    slot_index = jnp.sum(jnp.where(route_hot, earlier, 0.0), axis=1).astype(jnp.int32)
    chunk = (slot_index // quarter) ^ my_tensor
    place = (chunk * experts + chosen) * quarter + slot_index % quarter

    output_parts = gather_tensor(w_output)
    hidden, own, gate = call(
        hidden_kernel,
        "hidden",
        (((tok_rows, width), F32), ((chunk_rows, 2 * width), BF16), ((tok_rows, TILE), F32)),
        (my_tensor.astype(jnp.int32).reshape(1, 1),),
        (
            place[None, :], tokens, gather_tensor(after(mixed, output_parts[2])), output_parts, norm_second, router,
            routes, cotangent,
        ),
        scratch=(((tok_rows, 2 * width), BF16),),
    )
    arrived = exchange_expert(own.reshape(experts, quarter, 2 * width)).reshape(chunk_rows, 2 * width)
    forward, backward = arrived[:, :width], arrived[:, width:]
    forward_far, backward_far = swap(forward, "tensor", 2), swap(backward, "tensor", 2)
    forward_near, backward_near = swap(forward, "tensor", 1), swap(backward, "tensor", 1)

    keep_a, send_a, kept_result, send_result, active_a, pre_a, router_a = expert_pair(
        my_expert, (forward, backward), (forward_near, backward_near), weight_in, weight_out, router
    )
    forward_diag = swap(after(forward_far, active_a), "tensor", 1)
    backward_diag = swap(after(backward_far, active_a), "tensor", 1)
    got_a = swap(send_a, "tensor", 1)
    keep_b, send_b, far_result, far_send, active_b, pre_b, router_b = expert_pair(
        my_expert, (forward_far, backward_far), (forward_diag, backward_diag), weight_in, weight_out, router
    )
    other = (keep_b + swap(send_b, "tensor", 1).astype(F32)).astype(BF16)
    other_back = swap(other, "tensor", 2)

    own_back = ((keep_a + got_a.astype(F32)) + other_back.astype(F32)).astype(BF16)
    home = exchange_expert(own_back.reshape(experts, quarter, width)).reshape(chunk_rows, width)

    far_result = (far_result + swap(after(far_send, other), "tensor", 1).astype(F32)).astype(BF16)
    kept_result = kept_result + swap(after(send_result, other), "tensor", 1).astype(F32)
    other_result = swap(after(far_result, own_back), "tensor", 2)
    grad_expert_in, grad_expert_out = call(
        expert_grad_kernel,
        "expert_grads",
        ((weight_in.shape, F32), (weight_out.shape, F32)),
        (),
        (
            forward, forward_near, forward_far, forward_diag, backward, backward_near, backward_far, backward_diag,
            after(active_a, own_back), active_b, pre_a, pre_b,
        ),
    )
    own_result = (kept_result + other_result.astype(F32)).astype(BF16)
    home = after(home, (own_result, grad_expert_in))
    home_far = swap(home, "tensor", 2)
    returned_back = (home, swap(home, "tensor", 1), home_far, swap(home_far, "tensor", 1))

    grad_hidden, grad_mixed, turned, norm_part, output_sums = call(
        functools.partial(hidden_back_kernel, devices),
        "hidden_back",
        (
            ((tok_rows, width), F32), ((tok_rows, columns), BF16), ((columns, tok_rows), BF16), ((8, width), F32),
            ((width // 4, 4 * columns) if paired else (width, columns), BF16),
        ),
        (),
        (place[:, None], hidden, *returned_back, cotangent, norm_second, w_output, mixed),
        scratch=(((tok_rows, width), BF16),),
    )

    own_result = own_result.reshape(experts, quarter, width)
    if paired:
        both = exchange_expert(
            jnp.concatenate([own_result, output_sums.reshape(experts, quarter, width)], axis=1)
        )
        result, output_sums = both[:, :quarter].reshape(chunk_rows, width), both[:, quarter:]
    else:
        result = exchange_expert(own_result).reshape(chunk_rows, width)
        both = output_sums = exchange_expert(output_sums.reshape(devices, -1, columns))
    sums, keep, send, small = call(
        functools.partial(back_kernel, heads_here, columns // heads_here, devices),
        "layer_back",
        (
            ((3 * width // 4 + devices * (experts + 8), 4 * columns) if paired else (width, 3 * columns), BF16),
            ((half, width), F32), ((half, width), BF16), ((experts + 8, width), F32),
        ),
        (table, core.reshape(1, 1)),
        (
            queries, keys, values, grad_mixed, turned, totals, tokens, norm_first, *weights,
            router_a, router_b, norm_part,
        ),
        scratch=(
            ((2 * columns, tok_rows), F32), ((2 * columns, tok_rows), BF16), ((tok_rows, width), F32),
            ((tok_rows, width), BF16), ((tok_rows, columns), BF16),
        ),
    )
    sums, keep, send, small = lax.optimization_barrier((sums, keep, send, small, both))[:4]

    sums = exchange_expert(sums.reshape(devices, -1, sums.shape[1]))

    pair = (keep + swap(send, "tensor", 1).astype(F32)).astype(BF16)
    total = (pair.astype(F32) + swap(pair, "tensor", 2).astype(F32)).astype(BF16)
    result_far = swap(after(result, total), "tensor", 2)

    grads = jnp.sum(sums.astype(F32), axis=0)
    grad_output = jnp.sum(output_sums.astype(F32), axis=0)
    if paired:
        split = width // PAIRED // 2
        small = grads[3 * split // 2 :]
        grads = jnp.concatenate([unpacked(grads[:split], 2), unpacked(grads[split : 3 * split // 2], 4)], axis=1)
        grad_output = unpacked(grad_output, 4)
    else:
        small = sum_expert(small)

    near = swap(total, "tensor", 1)
    low = jnp.where(core == 1, near, total).astype(F32)
    high = jnp.where(core == 1, total, near).astype(F32)
    normed_back = jnp.concatenate([low, high])
    inputs = tokens.astype(F32)
    grad_tokens = grad_hidden + rms_norm_back(
        inputs, inv_rms_of(inputs), norm_first.astype(F32)[None, :], normed_back
    )

    returned = (result, swap(after(result, total), "tensor", 1), result_far, swap(result_far, "tensor", 1))
    place_hot = (
        place[:, None] == jnp.arange(TENSOR * chunk_rows, dtype=jnp.int32)[None, :]
    ).astype(BF16)
    layer_out = (hidden + gate[:, :1] * dot(place_hot, jnp.concatenate(returned))).astype(BF16)

    summed = small[: experts + 1]
    summed = after(summed, result_far)
    summed = summed + swap(summed, "tensor", 1)
    summed = summed + swap(summed, "tensor", 2)
    bias_size = BUCKETS * heads_here
    return (
        layer_out,
        grad_tokens,
        summed[experts],
        grads[:, :columns],
        grads[:, columns : 2 * columns],
        grads[:, 2 * columns :],
        grad_output.T,
        small[experts + 2, :bias_size].reshape(heads_here, BUCKETS).T,
        small[experts + 1],
        summed[:experts].T,
        grad_expert_in[None],
        grad_expert_out[None],
    )


def solution(mesh):
    return jax.shard_map(
        on_device,
        mesh=mesh,
        in_specs=(
            P("expert", None),
            P(),
            P(None, "tensor"),
            P(None, "tensor"),
            P(None, "tensor"),
            P("tensor", None),
            P(None, "tensor"),
            P(),
            P(),
            P("expert", None, "tensor"),
            P("expert", "tensor", None),
            P("expert", None),
            P("expert", None),
        ),
        out_specs=(
            P("expert", None),
            P("expert", None),
            P(),
            P("expert", "tensor"),
            P("expert", "tensor"),
            P("expert", "tensor"),
            P("tensor", "expert"),
            P(None, "tensor"),
            P(),
            P(),
            P("expert", None, "tensor"),
            P("expert", "tensor", None),
        ),
        check_vma=False,
    )
```

```python
import functools

import jax
import jax.numpy as jnp
from jax import lax
from jax.experimental import pallas as pl
from jax.experimental.pallas import tpu as pltpu
from jax.sharding import PartitionSpec as P

BUCKETS = 32
LEN = 512
TENSOR = 4
PAIRED = 8

EPSILON = 1e-06
THRESHOLDS = (12, 16, 23, 32, 46, 64, 91)
BF16 = jnp.bfloat16
F32 = jnp.float32
GELU_SCALE = (2.0 / 3.141592653589793) ** 0.5
GELU_CUBE = 0.044715
MIB = 1024 * 1024


def dot(left, right):
    return jnp.dot(left, right, preferred_element_type=F32)


def dot_t(left, right):
    return lax.dot_general(left, right, (((1,), (1,)), ((), ())), preferred_element_type=F32)


def t_dot(left, right):
    return lax.dot_general(left, right, (((0,), (0,)), ((), ())), preferred_element_type=F32)


def inv_rms_of(values):
    return lax.rsqrt(jnp.mean(values * values, axis=-1, keepdims=True) + EPSILON)


def rms_norm_back(values, inv_rms, gain, grad):
    scaled = gain * grad
    inner = jnp.mean(scaled * values, axis=-1, keepdims=True)
    return inv_rms * scaled - values * (inv_rms * inv_rms * inv_rms * inner)


TILE = 128


def skew(tile):
    return pltpu.roll(tile, 0, 1, stride=1, stride_axis=0)


def diagonal_sums(tile):
    row = lax.broadcasted_iota(jnp.int32, (TILE, TILE), 0)
    turn = (row + lax.broadcasted_iota(jnp.int32, (TILE, TILE), 1) == TILE - 1).astype(F32)
    turned = lax.dot_general(
        turn, tile, (((1,), (0,)), ((), ())), precision=lax.Precision.HIGHEST, preferred_element_type=F32
    )
    return jnp.sum(pltpu.roll(turned, 1, 1, stride=1, stride_axis=0), axis=0, keepdims=True)


def bias_tiles(table_ref, head):
    lane = lax.broadcasted_iota(jnp.int32, (8, TILE), 1)
    place = lax.broadcasted_iota(jnp.int32, (TILE, TILE), 1)

    def chain(base, distance):
        line = jnp.full((8, TILE), table_ref[head, base], F32)
        for n in range(1, 8):
            line = jnp.where(distance >= n, table_ref[head, base + n], line)
        for n, threshold in enumerate((8,) + THRESHOLDS):
            line = jnp.where(distance >= threshold, table_ref[head, base + 8 + n], line)
        return jnp.broadcast_to(line[0:1, :], (TILE, TILE))

    ahead = skew(jnp.where(place == 0, table_ref[head, 0], chain(16, lane)))
    behind = skew(chain(0, TILE - lane))
    upper = place >= lax.broadcasted_iota(jnp.int32, (TILE, TILE), 0)
    return [
        jnp.where(upper, behind, table_ref[head, 15]),
        jnp.where(upper, ahead, behind),
        jnp.where(upper, table_ref[head, 31], ahead),
    ]


def bias_rows(table_ref, tiles, head, block):
    parts = []
    for other in range(LEN // TILE):
        offset = other - block
        if offset < -1:
            parts.append(jnp.full((TILE, TILE), table_ref[head, 15], F32))
        elif offset > 1:
            parts.append(jnp.full((TILE, TILE), table_ref[head, 31], F32))
        else:
            parts.append(tiles[offset + 1])
    return jnp.concatenate(parts, axis=1)


def head_columns(values, head, size):
    lane = lax.broadcasted_iota(jnp.int32, values.shape, 1)
    return jnp.where((lane >= head * size) & (lane < (head + 1) * size), values, jnp.zeros_like(values))


def attend_kernel(heads, size, table_ref, tokens_ref, gain_ref, wq_ref, wk_ref, wv_ref, q_ref, k_ref, v_ref, mixed_ref, total_ref):
    values = tokens_ref[...].astype(F32)
    normed = (values * inv_rms_of(values) * gain_ref[...].astype(F32).reshape(1, -1)).astype(BF16)
    q_ref[...] = dot_t(normed, wq_ref[...]).astype(BF16)
    q_ref.leave()
    k_ref[...] = dot_t(normed, wk_ref[...]).astype(BF16)
    k_ref.leave()
    v_ref[...] = dot_t(normed, wv_ref[...]).astype(BF16)
    v_ref.leave()
    all_tiles = [bias_tiles(table_ref, head) for head in range(heads)]
    keys = k_ref[...]
    head_values = [head_columns(v_ref[...], head, size) for head in range(heads)]
    for block in range(LEN // TILE):
        rows = pl.ds(block * TILE, TILE)
        queries = q_ref[rows, :]
        mixed = None
        lane = lax.broadcasted_iota(jnp.int32, (TILE, TILE), 1)
        totals = jnp.zeros((TILE, TILE), F32)
        for head in range(heads):
            scores = dot_t(head_columns(queries, head, size), keys)
            scores = scores + bias_rows(table_ref, all_tiles[head], head, block)
            row_max = jnp.max(scores, axis=-1, keepdims=True)
            exponent = jnp.exp(scores - row_max)
            row_total = jnp.sum(exponent, axis=-1, keepdims=True)
            weights = (exponent * (1.0 / row_total)).astype(BF16)
            part = dot(weights, head_values[head])
            mixed = part if mixed is None else mixed + part
            totals = jnp.where(lane == head, row_max + jnp.log(row_total), totals)
        mixed_ref[rows, :] = mixed.astype(BF16)
        total_ref[rows, :] = totals


class Input:
    def __init__(self, copies, buffer):
        self.copies, self.buffer, self.shape = copies, buffer, buffer.shape
        self.begun, self.later = False, ()

    def begin(self):
        if not self.begun:
            for copy in self.copies:
                copy.start()
        self.begun = True

    def land(self):
        self.begin()
        for copy in self.copies:
            copy.wait()
        self.copies = ()
        for entry in self.later:
            entry.begin()
        self.later = ()

    def __getitem__(self, index):
        self.land()
        return self.buffer[index]


class Output:
    def __init__(self, copy, buffer):
        self.copy, self.buffer, self.shape, self.left = copy, buffer, buffer.shape, False

    def __getitem__(self, index):
        return self.buffer[index]

    def __setitem__(self, index, values):
        self.buffer[index] = values

    def leave(self):
        if not self.left:
            self.copy.start()
        self.left = True


def call(kernel, name, outs, smem, operands, scratch=(), first=None, limit=60, flops=10**5, moved=10**4):
    groups = [entry if isinstance(entry, tuple) else (entry,) for entry in operands]
    arrays = [array for group in groups for array in group]
    anywhere = pl.BlockSpec(memory_space=pl.ANY)
    held = [
        pltpu.VMEM((len(group),) * (len(group) > 1) + group[0].shape, group[0].dtype) for group in groups
    ] + [pltpu.VMEM(shape, kind) for shape, kind in outs]

    def body(*refs):
        refs = list(refs)

        def take(count):
            taken = refs[:count]
            del refs[:count]
            return taken

        scalars, sources, targets = take(len(smem)), take(len(arrays)), take(len(outs))
        in_buffers, out_buffers = take(len(groups)), take(len(outs))
        in_sems, out_sems = take(2)
        inputs, number = [], 0
        for group, buffer in zip(groups, in_buffers):
            copies = []
            for m in range(len(group)):
                place = buffer if len(group) == 1 else buffer.at[scalars[0][0, 0] ^ m]
                copies.append(pltpu.make_async_copy(sources[number], place, in_sems.at[number]))
                number += 1
            inputs.append(Input(copies, buffer))
        for entry in inputs[:first]:
            entry.begin()
            entry.later = inputs[len(inputs) if first is None else first :]
        outputs = [
            Output(pltpu.make_async_copy(buffer, target, out_sems.at[i]), buffer)
            for i, (buffer, target) in enumerate(zip(out_buffers, targets))
        ]
        kernel(*scalars, *inputs, *outputs, *refs)
        for entry in inputs:
            entry.land()
        for entry in outputs:
            entry.leave()
        for entry in outputs:
            entry.copy.wait()

    return pl.pallas_call(
        body,
        out_shape=tuple(jax.ShapeDtypeStruct(shape, kind) for shape, kind in outs),
        in_specs=[pl.BlockSpec(memory_space=pltpu.SMEM)] * len(smem) + [anywhere] * len(arrays),
        out_specs=(anywhere,) * len(outs),
        scratch_shapes=held
        + [pltpu.SemaphoreType.DMA((len(arrays),)), pltpu.SemaphoreType.DMA((len(outs),))]
        + [pltpu.VMEM(shape, kind) for shape, kind in scratch],
        compiler_params=pltpu.CompilerParams(vmem_limit_bytes=limit * MIB),
        cost_estimate=pl.CostEstimate(flops=flops, bytes_accessed=moved, transcendentals=0),
        name=name,
    )(*smem, *arrays)


def attend(tokens, gains, weights, table, heads):
    rows, columns = tokens.shape[0], weights[0].shape[0]
    small = ((rows, columns), BF16)
    return call(
        functools.partial(attend_kernel, heads, columns // heads),
        "attend",
        (small, small, small, small, ((rows, TILE), F32)),
        (table,),
        (tokens, gains, *weights),
    )


def hidden_kernel(tensor_ref, place_ref, tokens_ref, mixed_ref, weight_ref, gain_ref, router_ref, routes_ref, cot_ref, hidden_ref, own_ref, gate_ref, both):
    width = tokens_ref.shape[1]
    experts = router_ref.shape[0]
    gain = gain_ref[...].astype(F32).reshape(1, -1)
    for block in range(tokens_ref.shape[0] // TILE):
        rows = pl.ds(block * TILE, TILE)
        hidden = tokens_ref[rows, :].astype(F32)
        for m in range(TENSOR):
            hidden = hidden + dot(mixed_ref[m, rows, :], weight_ref[m])
        hidden_ref[rows, :] = hidden
        normed = (hidden * inv_rms_of(hidden) * gain).astype(BF16)
        probs = softmax(dot_t(normed, router_ref[...]))
        lane = lax.broadcasted_iota(jnp.int32, (TILE, experts), 1)
        gate = jnp.sum(jnp.where(lane == routes_ref[rows, :], probs, 0.0), axis=-1, keepdims=True)
        gate_ref[rows, :] = jnp.broadcast_to(gate, (TILE, TILE))
        both[rows, :width] = normed
        both[rows, width:] = (cot_ref[rows, :].astype(F32) * gate).astype(BF16)
    hidden_ref.leave()
    gate_ref.leave()
    slots = own_ref.shape[0]
    row = lax.broadcasted_iota(jnp.int32, (slots, place_ref.shape[1]), 0)
    own_ref[...] = dot((row == place_ref[...]).astype(BF16), both[...]).astype(BF16)


def softmax(values):
    exponent = jnp.exp(values - jnp.max(values, axis=-1, keepdims=True))
    return exponent / jnp.sum(exponent, axis=-1, keepdims=True)


def expert_kernel(me_ref, f_b, in_ref, b_b, out_ref, router_ref, f_a, b_a, keep_ref, send_ref, keep_r_ref, send_r_ref, active_ref, pre_ref, grad_ref):
    rows = f_a.shape[0]
    experts = router_ref.shape[0]
    lane = lax.broadcasted_iota(jnp.int32, (rows, experts), 1)
    own_hot = (lane == me_ref[0, 0]).astype(F32)
    total = None
    for place, (forward, backward) in enumerate(((f_b, b_b), (f_a, b_a))):
        pre = dot(forward[...], in_ref[...])
        square = pre * pre
        bent = jnp.tanh(GELU_SCALE * (pre + GELU_CUBE * square * pre))
        active = (0.5 * pre * (1.0 + bent)).astype(BF16)
        slope = 0.5 * (1.0 + bent) + 0.5 * pre * (1.0 - bent * bent) * (
            GELU_SCALE * (1.0 + 3.0 * GELU_CUBE * square)
        )
        grad_active = dot_t(backward[...], out_ref[...])
        grad_pre = (grad_active * slope).astype(BF16)
        gate_grad = jnp.sum(active.astype(F32) * grad_active, axis=1, keepdims=True)
        probs = softmax(dot_t(forward[...], router_ref[...]))
        grad_logits = (gate_grad * (own_hot - probs)).astype(BF16)
        back = dot_t(grad_pre, in_ref[...]) + dot(grad_logits, router_ref[...])
        where = pl.ds((1 - place) * rows, rows)
        active_ref[where, :] = active
        pre_ref[where, :] = grad_pre
        if place == 0:
            send_ref[...] = back.astype(BF16)
            send_ref.leave()
            send_r_ref[...] = dot(active, out_ref[...]).astype(BF16)
            send_r_ref.leave()
        else:
            keep_ref[...] = back
            keep_ref.leave()
            keep_r_ref[...] = dot(active, out_ref[...])
        part = t_dot(grad_logits, forward[...])
        total = part if total is None else total + part
    grad_ref[...] = total


def expert_pair(me, first, second, weight_in, weight_out, router):
    rows, width = first[0].shape
    hidden = weight_in.shape[1]
    return call(
        expert_kernel,
        "expert_pair",
        (
            ((rows, width), F32), ((rows, width), BF16), ((rows, width), F32), ((rows, width), BF16),
            ((2 * rows, hidden), BF16), ((2 * rows, hidden), BF16),
            (router.shape, F32),
        ),
        (me,),
        (second[0], weight_in, second[1], weight_out, router, *first),

    )


def expert_grad_kernel(f0, f1, f2, f3, b0, b1, b2, b3, active_a, active_b, pre_a, pre_b, in_ref, out_ref):
    rows = f0.shape[0]
    forward = jnp.concatenate([f0[...], f1[...], f2[...], f3[...]], axis=0)
    pre = jnp.concatenate([pre_a[...], pre_b[...]], axis=0)
    in_ref[...] = t_dot(forward, pre)
    backward = jnp.concatenate([b0[...], b1[...], b2[...], b3[...]], axis=0)
    active = jnp.concatenate([active_a[...], active_b[...]], axis=0)
    out_ref[...] = t_dot(active, backward)


def packed(rows, count):
    size = rows.shape[0] // count
    return jnp.concatenate([rows[n * size : (n + 1) * size] for n in range(count)], axis=1)


def unpacked(rows, count):
    size = rows.shape[1] // count
    return jnp.concatenate([rows[:, n * size : (n + 1) * size] for n in range(count)], axis=0)


def hidden_back_kernel(
    devices, place_ref, hidden_ref, r0, r1, r2, r3, cot_ref, gain_ref, wo_ref, mixed_ref,
    router_a, router_b, grad_ref, gm_ref, turned_ref, norm_ref, sums_ref, router_ref, attn_ref,
):
    tok_rows, width = hidden_ref.shape
    columns = mixed_ref.shape[1]
    chunk = r0.shape[0]
    gain = gain_ref[...].astype(F32).reshape(1, -1)
    norm_part = None
    for block in range(tok_rows // TILE):
        rows = pl.ds(block * TILE, TILE)
        place = place_ref[rows, :]
        back = None
        for m, returned in enumerate((r0, r1, r2, r3)):
            lane = lax.broadcasted_iota(jnp.int32, (TILE, chunk), 1) + m * chunk
            found = dot((lane == place).astype(BF16), returned[...])
            back = found if back is None else back + found
        hidden = hidden_ref[rows, :]
        inv = inv_rms_of(hidden)
        summed = jnp.sum((back * hidden * inv).reshape(TILE // 8, 8, width), axis=0)
        norm_part = summed if norm_part is None else norm_part + summed
        grad = cot_ref[rows, :].astype(F32) + rms_norm_back(hidden, inv, gain, back)
        grad_ref[rows, :] = grad
        low = grad.astype(BF16)
        attn_ref[rows, :] = low
        gm_ref[rows, :] = dot_t(low, wo_ref[...]).astype(BF16)
    grad_ref.leave()
    gm_ref.leave()
    unit = lax.broadcasted_iota(jnp.int32, (columns, columns), 0)
    unit = (unit == lax.broadcasted_iota(jnp.int32, (columns, columns), 1)).astype(BF16)
    sums = dot(dot_t(unit, mixed_ref[...]).astype(BF16), attn_ref[...]).T
    router = router_a[...] + router_b[...]
    router_ref[...] = router
    if devices == PAIRED:
        size = width // devices
        blocks = [packed(sums[n * size : (n + 1) * size], 4) for n in range(devices)]
        sums = jnp.concatenate([piece for block in blocks for piece in (block, router)], axis=0)
    sums_ref[...] = sums.astype(BF16)
    sums_ref.leave()
    turned_ref[...] = dot_t(wo_ref[...], attn_ref[...]).astype(BF16)
    norm_ref[...] = norm_part


def back_kernel(
    heads, size, devices, table_ref, core_ref, q_ref, k_ref, v_ref, gm_ref, turned_ref, total_ref,
    tokens_ref, gain_ref, wq_ref, wk_ref, wv_ref, norm_ref,
    sums_ref, keep_ref, send_ref, small_ref, back_t, turn_t, part_ref, normed_ref, qb_ref,
):
    tok_rows, width = tokens_ref.shape
    columns = q_ref.shape[1]
    count = LEN // TILE
    keys, all_values = k_ref[...], v_ref[...]
    back_t[...] = jnp.zeros_like(back_t)
    unit = lax.broadcasted_iota(jnp.int32, (columns, columns), 0)
    unit = (unit == lax.broadcasted_iota(jnp.int32, (columns, columns), 1)).astype(BF16)
    turn_t[pl.ds(0, columns), :] = dot_t(unit, q_ref[...]).astype(BF16)
    turn_t[pl.ds(columns, columns), :] = turned_ref[...]
    all_tiles = [bias_tiles(table_ref, head) for head in range(heads)]
    head_keys = [head_columns(keys, head, size) for head in range(heads)]
    near = [[None] * 3 for _ in range(heads)]
    far = [[None] * 2 for _ in range(heads)]
    for block in range(count):
        rows = pl.ds(block * TILE, TILE)
        queries, grads, totals = q_ref[rows, :], gm_ref[rows, :], total_ref[rows, :]
        query_back = None
        for head in range(heads):
            head_queries = head_columns(queries, head, size)
            head_grads = head_columns(grads, head, size)
            scores = dot_t(head_queries, keys)
            scores = scores + bias_rows(table_ref, all_tiles[head], head, block)
            probs = jnp.exp(scores - totals[:, head : head + 1])
            probs_grad = dot_t(head_grads, all_values)
            inner = jnp.sum(probs_grad * probs, axis=-1, keepdims=True)
            score_grad = (probs * (probs_grad - inner)).astype(BF16)
            part = dot(score_grad, head_keys[head])
            query_back = part if query_back is None else query_back + part
            mine = pl.ds(head * size, size)
            back_t[mine, :] += dot(turn_t[mine, rows], score_grad)
            mine = pl.ds(columns + head * size, size)
            back_t[mine, :] += dot(turn_t[mine, rows], probs.astype(BF16))
            wide = score_grad.astype(F32)
            for other in range(count):
                offset = other - block
                tile = wide[:, other * TILE : (other + 1) * TILE]
                if abs(offset) <= 1:
                    held = near[head][offset + 1]
                    near[head][offset + 1] = tile if held is None else held + tile
                else:
                    side = 0 if offset < 0 else 1
                    summed = jnp.sum(tile.reshape(TILE // 8, 8, TILE), axis=0)
                    held = far[head][side]
                    far[head][side] = summed if held is None else held + summed
        qb_ref[rows, :] = query_back.astype(BF16)
    inputs = tokens_ref[...].astype(F32)
    inv_first = inv_rms_of(inputs)
    normed_ref[...] = (inputs * inv_first * gain_ref[...].astype(F32).reshape(1, -1)).astype(BF16)
    query_back = qb_ref[...]
    key_t = back_t[pl.ds(0, columns), :].astype(BF16)
    value_t = back_t[pl.ds(columns, columns), :].astype(BF16)
    part_ref[...] = dot(query_back, wq_ref[...]) + t_dot(key_t, wk_ref[...]) + t_dot(value_t, wv_ref[...])
    half = tok_rows // 2
    core = core_ref[0, 0]
    keep_ref[...] = part_ref[pl.ds(pl.multiple_of(core * half, half), half), :]
    keep_ref.leave()
    send_ref[...] = part_ref[pl.ds(pl.multiple_of((1 - core) * half, half), half), :].astype(BF16)
    send_ref.leave()
    bias_row = jnp.concatenate([bias_sums(heads, near, far), jnp.zeros((8, width - TILE), F32)], axis=1)
    norm_row = jnp.broadcast_to(jnp.sum(norm_ref[...], axis=0, keepdims=True), (8, width))
    first_part = jnp.sum(part_ref[...] * tokens_ref[...].astype(F32) * inv_first, axis=0, keepdims=True)
    line = lax.broadcasted_iota(jnp.int32, (8, width), 0)
    lines = jnp.where(line == 0, first_part, jnp.where(line == 1, norm_row, jnp.where(line == 2, bias_row, 0.0)))
    small = lines
    small_ref[...] = small
    small_ref.leave()
    turned = (dot_t(unit, query_back).astype(BF16), key_t, value_t)
    parts = [dot(rows, normed_ref[...]) for rows in turned]
    sums = jnp.concatenate(parts, axis=0).T
    if devices == PAIRED:
        size = width // devices
        blocks = [sums[n * size : (n + 1) * size] for n in range(devices)]
        sums = jnp.concatenate(
            [
                piece
                for block in blocks
                for piece in (packed(block[:, : 2 * columns], 2), packed(block[:, 2 * columns :], 4), small)
            ],
            axis=0,
        )
    sums_ref[...] = sums.astype(BF16)
    sums_ref.leave()


def bias_sums(heads, near, far):
    upper = lax.broadcasted_iota(jnp.int32, (TILE, TILE), 1) >= lax.broadcasted_iota(jnp.int32, (TILE, TILE), 0)
    edges = tuple(range(8)) + (8,) + THRESHOLDS + (1 << 20,)
    lane = lax.broadcasted_iota(jnp.int32, (TILE, TILE), 0)
    place = lax.broadcasted_iota(jnp.int32, (TILE, TILE), 1)
    total = jnp.zeros((8, TILE), F32)

    def bucket(distance):
        found = jnp.zeros((TILE, TILE), jnp.int32)
        for n in range(1, 16):
            found = jnp.where(distance >= edges[n], n, found)
        return found

    for head in range(heads):
        before, here, beyond = near[head]
        start = head * BUCKETS
        ahead = diagonal_sums(jnp.where(upper, here, beyond))
        behind = diagonal_sums(jnp.where(upper, before, here))
        outside = (
            jnp.sum(jnp.where(upper, 0.0, before), axis=0, keepdims=True) + jnp.sum(far[head][0], axis=0, keepdims=True),
            jnp.sum(jnp.where(upper, beyond, 0.0), axis=0, keepdims=True) + jnp.sum(far[head][1], axis=0, keepdims=True),
        )
        targets = (
            start + jnp.where(lane == 0, 0, 16 + bucket(lane)),
            start + bucket(TILE - lane),
            jnp.full((TILE, TILE), start + 15, jnp.int32),
            jnp.full((TILE, TILE), start + 31, jnp.int32),
        )
        for row, target in zip((ahead, behind, *outside), targets):
            total = total + lax.dot_general(
                jnp.broadcast_to(row, (8, TILE)), (place == target).astype(F32), (((1,), (0,)), ((), ())),
                precision=lax.Precision.HIGHEST, preferred_element_type=F32,
            )
    return total


def swap(values, axis, mask):
    size = lax.axis_size(axis)
    return lax.ppermute(values, axis, [(i, i ^ mask) for i in range(size)])


def gather_tensor(values):
    far = swap(values, "tensor", 2)
    near = swap(values, "tensor", 1)
    return values, near, far, swap(far, "tensor", 1)


def exchange_expert(blocks):
    return lax.all_to_all(blocks, "expert", split_axis=0, concat_axis=0, tiled=True)


def after(values, done):
    return lax.optimization_barrier((values, done))[0]


def sum_expert(values):
    mask = 1
    while mask < lax.axis_size("expert"):
        values = values + swap(values, "expert", mask)
        mask = 2 * mask
    return values


def on_device(
    tokens,
    norm_first,
    w_query,
    w_key,
    w_value,
    w_output,
    bias_table,
    norm_second,
    w_router,
    w_expert_in,
    w_expert_out,
    routes,
    cotangent,
):
    tok_rows, width = tokens.shape
    experts = w_router.shape[1]
    capacity = max(2, 3 * tok_rows // (2 * experts))
    quarter = -(-capacity // TENSOR)
    heads_here = bias_table.shape[1]
    columns = w_query.shape[1]
    chunk_rows = experts * quarter
    half = tok_rows // 2
    devices = lax.axis_size("expert")
    paired = devices == PAIRED
    my_tensor = lax.axis_index("tensor")
    my_expert = lax.axis_index("expert").astype(jnp.int32).reshape(1, 1)
    core = (my_tensor & 1).astype(jnp.int32)
    weight_in = w_expert_in[0]
    weight_out = w_expert_out[0]
    router = w_router.T
    weights = (w_query.T, w_key.T, w_value.T)
    table = bias_table.T.astype(F32)

    queries, keys, values, mixed, totals = attend(tokens, norm_first, weights, table, heads_here)

    chosen = routes[:, 0]
    route_hot = chosen[:, None] == jnp.arange(experts, dtype=jnp.int32)[None, :]
    places = jnp.arange(tok_rows, dtype=jnp.int32)
    before = (places[:, None] > places[None, :]).astype(BF16)
    earlier = dot(before, route_hot.astype(BF16))
    slot_index = jnp.sum(jnp.where(route_hot, earlier, 0.0), axis=1).astype(jnp.int32)
    chunk = (slot_index // quarter) ^ my_tensor
    place = (chunk * experts + chosen) * quarter + slot_index % quarter

    output_parts = gather_tensor(w_output)
    hidden, own, gate = call(
        hidden_kernel,
        "hidden",
        (((tok_rows, width), F32), ((chunk_rows, 2 * width), BF16), ((tok_rows, TILE), F32)),
        (my_tensor.astype(jnp.int32).reshape(1, 1),),
        (
            place[None, :], tokens, gather_tensor(after(mixed, output_parts[2])), output_parts, norm_second, router,
            routes, cotangent,
        ),
        scratch=(((tok_rows, 2 * width), BF16),),
    )
    arrived = exchange_expert(own.reshape(experts, quarter, 2 * width)).reshape(chunk_rows, 2 * width)
    forward, backward = arrived[:, :width], arrived[:, width:]
    forward_far, backward_far = swap(forward, "tensor", 2), swap(backward, "tensor", 2)
    forward_near, backward_near = swap(forward, "tensor", 1), swap(backward, "tensor", 1)

    keep_a, send_a, kept_result, send_result, active_a, pre_a, router_a = expert_pair(
        my_expert, (forward, backward), (forward_near, backward_near), weight_in, weight_out, router
    )
    forward_diag = swap(after(forward_far, active_a), "tensor", 1)
    backward_diag = swap(after(backward_far, active_a), "tensor", 1)
    got_a = swap(send_a, "tensor", 1)
    keep_b, send_b, far_result, far_send, active_b, pre_b, router_b = expert_pair(
        my_expert, (forward_far, backward_far), (forward_diag, backward_diag), weight_in, weight_out, router
    )
    other = (keep_b + swap(send_b, "tensor", 1).astype(F32)).astype(BF16)
    other_back = swap(other, "tensor", 2)

    own_back = ((keep_a + got_a.astype(F32)) + other_back.astype(F32)).astype(BF16)
    home = exchange_expert(own_back.reshape(experts, quarter, width)).reshape(chunk_rows, width)

    far_result = (far_result + swap(after(far_send, other), "tensor", 1).astype(F32)).astype(BF16)
    kept_result = kept_result + swap(after(send_result, other), "tensor", 1).astype(F32)
    other_result = swap(after(far_result, own_back), "tensor", 2)
    grad_expert_in, grad_expert_out = call(
        expert_grad_kernel,
        "expert_grads",
        ((weight_in.shape, F32), (weight_out.shape, F32)),
        (),
        (
            forward, forward_near, forward_far, forward_diag, backward, backward_near, backward_far, backward_diag,
            after(active_a, own_back), active_b, pre_a, pre_b,
        ),
    )
    own_result = (kept_result + other_result.astype(F32)).astype(BF16)
    home = after(home, (own_result, grad_expert_in))
    home_far = swap(home, "tensor", 2)
    returned_back = (home, swap(home, "tensor", 1), home_far, swap(home_far, "tensor", 1))

    result = exchange_expert(after(own_result, home).reshape(experts, quarter, width)).reshape(chunk_rows, width)

    grad_hidden, grad_mixed, turned, norm_part, output_sums, router_part = call(
        functools.partial(hidden_back_kernel, devices),
        "hidden_back",
        (
            ((tok_rows, width), F32), ((tok_rows, columns), BF16), ((columns, tok_rows), BF16), ((8, width), F32),
            ((width // 4 + devices * experts, 4 * columns) if paired else (width, columns), BF16),
            (router.shape, F32),
        ),
        (),
        (place[:, None], hidden, *returned_back, cotangent, norm_second, w_output, mixed, router_a, router_b),
        scratch=(((tok_rows, width), BF16),),
    )

    grad_hidden, grad_mixed, turned, norm_part, output_sums, _ = lax.optimization_barrier(
        (grad_hidden, grad_mixed, turned, norm_part, output_sums, result)
    )

    output_sums = exchange_expert(output_sums.reshape(devices, -1, output_sums.shape[1]))
    result_far = swap(result, "tensor", 2)
    sums, keep, send, small = call(
        functools.partial(back_kernel, heads_here, columns // heads_here, devices),
        "layer_back",
        (
            ((3 * width // 4 + devices * 8, 4 * columns) if paired else (width, 3 * columns), BF16),
            ((half, width), F32), ((half, width), BF16), ((8, width), F32),
        ),
        (table, core.reshape(1, 1)),
        (
            queries, keys, values, grad_mixed, turned, totals, tokens, norm_first, *weights, norm_part,
        ),
        first=6,
        scratch=(
            ((2 * columns, tok_rows), F32), ((2 * columns, tok_rows), BF16), ((tok_rows, width), F32),
            ((tok_rows, width), BF16), ((tok_rows, columns), BF16),
        ),
    )
    sums, keep, send, small = lax.optimization_barrier((sums, keep, send, small, output_sums, result_far))[:4]

    sums = exchange_expert(sums.reshape(devices, -1, sums.shape[1]))

    pair = (keep + swap(send, "tensor", 1).astype(F32)).astype(BF16)
    total = (pair.astype(F32) + swap(pair, "tensor", 2).astype(F32)).astype(BF16)

    grads = jnp.sum(sums.astype(F32), axis=0)
    grad_output = jnp.sum(output_sums.astype(F32), axis=0)
    if paired:
        split = width // PAIRED // 2
        small = grads[3 * split // 2 :]
        grads = jnp.concatenate([unpacked(grads[:split], 2), unpacked(grads[split : 3 * split // 2], 4)], axis=1)
        grad_router = grad_output[split // 2 :]
        grad_output = unpacked(grad_output[: split // 2], 4)
    else:
        small = sum_expert(small)
        grad_router = sum_expert(router_part)

    near = swap(total, "tensor", 1)
    low = jnp.where(core == 1, near, total).astype(F32)
    high = jnp.where(core == 1, total, near).astype(F32)
    normed_back = jnp.concatenate([low, high])
    inputs = tokens.astype(F32)
    grad_tokens = grad_hidden + rms_norm_back(
        inputs, inv_rms_of(inputs), norm_first.astype(F32)[None, :], normed_back
    )

    returned = (result, swap(after(result, total), "tensor", 1), result_far, swap(result_far, "tensor", 1))
    place_hot = (
        place[:, None] == jnp.arange(TENSOR * chunk_rows, dtype=jnp.int32)[None, :]
    ).astype(BF16)
    layer_out = (hidden + gate[:, :1] * dot(place_hot, jnp.concatenate(returned))).astype(BF16)

    grad_router = grad_router + swap(after(grad_router, total), "tensor", 1)
    grad_router = grad_router + swap(grad_router, "tensor", 2)
    first = small + swap(small, "tensor", 1)
    first = first + swap(after(first, (result_far, grad_router)), "tensor", 2)
    bias_size = BUCKETS * heads_here
    return (
        layer_out,
        grad_tokens,
        first[0],
        grads[:, :columns],
        grads[:, columns : 2 * columns],
        grads[:, 2 * columns :],
        grad_output.T,
        small[2, :bias_size].reshape(heads_here, BUCKETS).T,
        small[1],
        grad_router.T,
        grad_expert_in[None],
        grad_expert_out[None],
    )


def solution(mesh):
    return jax.shard_map(
        on_device,
        mesh=mesh,
        in_specs=(
            P("expert", None),
            P(),
            P(None, "tensor"),
            P(None, "tensor"),
            P(None, "tensor"),
            P("tensor", None),
            P(None, "tensor"),
            P(),
            P(),
            P("expert", None, "tensor"),
            P("expert", "tensor", None),
            P("expert", None),
            P("expert", None),
        ),
        out_specs=(
            P("expert", None),
            P("expert", None),
            P(),
            P("expert", "tensor"),
            P("expert", "tensor"),
            P("expert", "tensor"),
            P("tensor", "expert"),
            P(None, "tensor"),
            P(),
            P(),
            P("expert", None, "tensor"),
            P("expert", "tensor", None),
        ),
        check_vma=False,
    )
```

```python
import functools

import jax
import jax.numpy as jnp
from jax import lax
from jax.experimental import pallas as pl
from jax.experimental.pallas import tpu as pltpu
from jax.sharding import PartitionSpec as P

BUCKETS = 32
LEN = 512
TENSOR = 4
PAIRED = 8

EPSILON = 1e-06
THRESHOLDS = (12, 16, 23, 32, 46, 64, 91)
BF16 = jnp.bfloat16
F32 = jnp.float32
GELU_SCALE = (2.0 / 3.141592653589793) ** 0.5
GELU_CUBE = 0.044715
MIB = 1024 * 1024


def dot(left, right):
    return jnp.dot(left, right, preferred_element_type=F32)


def dot_t(left, right):
    return lax.dot_general(left, right, (((1,), (1,)), ((), ())), preferred_element_type=F32)


def t_dot(left, right):
    return lax.dot_general(left, right, (((0,), (0,)), ((), ())), preferred_element_type=F32)


def inv_rms_of(values):
    return lax.rsqrt(jnp.mean(values * values, axis=-1, keepdims=True) + EPSILON)


def rms_norm_back(values, inv_rms, gain, grad):
    scaled = gain * grad
    inner = jnp.mean(scaled * values, axis=-1, keepdims=True)
    return inv_rms * scaled - values * (inv_rms * inv_rms * inv_rms * inner)


TILE = 128


def skew(tile):
    return pltpu.roll(tile, 0, 1, stride=1, stride_axis=0)


def diagonal_sums(tile):
    row = lax.broadcasted_iota(jnp.int32, (TILE, TILE), 0)
    turn = (row + lax.broadcasted_iota(jnp.int32, (TILE, TILE), 1) == TILE - 1).astype(F32)
    turned = lax.dot_general(
        turn, tile, (((1,), (0,)), ((), ())), precision=lax.Precision.HIGHEST, preferred_element_type=F32
    )
    return jnp.sum(pltpu.roll(turned, 1, 1, stride=1, stride_axis=0), axis=0, keepdims=True)


def bias_tiles(table_ref, head):
    lane = lax.broadcasted_iota(jnp.int32, (8, TILE), 1)
    place = lax.broadcasted_iota(jnp.int32, (TILE, TILE), 1)

    def chain(base, distance):
        line = jnp.full((8, TILE), table_ref[head, base], F32)
        for n in range(1, 8):
            line = jnp.where(distance >= n, table_ref[head, base + n], line)
        for n, threshold in enumerate((8,) + THRESHOLDS):
            line = jnp.where(distance >= threshold, table_ref[head, base + 8 + n], line)
        return jnp.broadcast_to(line[0:1, :], (TILE, TILE))

    ahead = skew(jnp.where(place == 0, table_ref[head, 0], chain(16, lane)))
    behind = skew(chain(0, TILE - lane))
    upper = place >= lax.broadcasted_iota(jnp.int32, (TILE, TILE), 0)
    return [
        jnp.where(upper, behind, table_ref[head, 15]),
        jnp.where(upper, ahead, behind),
        jnp.where(upper, table_ref[head, 31], ahead),
    ]


def bias_rows(table_ref, tiles, head, block):
    parts = []
    for other in range(LEN // TILE):
        offset = other - block
        if offset < -1:
            parts.append(jnp.full((TILE, TILE), table_ref[head, 15], F32))
        elif offset > 1:
            parts.append(jnp.full((TILE, TILE), table_ref[head, 31], F32))
        else:
            parts.append(tiles[offset + 1])
    return jnp.concatenate(parts, axis=1)


def head_columns(values, head, size):
    lane = lax.broadcasted_iota(jnp.int32, values.shape, 1)
    return jnp.where((lane >= head * size) & (lane < (head + 1) * size), values, jnp.zeros_like(values))


def attend_kernel(heads, size, table_ref, tokens_ref, gain_ref, wq_ref, wk_ref, wv_ref, q_ref, k_ref, v_ref, mixed_ref, total_ref):
    values = tokens_ref[...].astype(F32)
    normed = (values * inv_rms_of(values) * gain_ref[...].astype(F32).reshape(1, -1)).astype(BF16)
    q_ref[...] = dot_t(normed, wq_ref[...]).astype(BF16)
    q_ref.leave()
    k_ref[...] = dot_t(normed, wk_ref[...]).astype(BF16)
    k_ref.leave()
    v_ref[...] = dot_t(normed, wv_ref[...]).astype(BF16)
    v_ref.leave()
    all_tiles = [bias_tiles(table_ref, head) for head in range(heads)]
    keys = k_ref[...]
    head_values = [head_columns(v_ref[...], head, size) for head in range(heads)]
    for block in range(LEN // TILE):
        rows = pl.ds(block * TILE, TILE)
        queries = q_ref[rows, :]
        mixed = None
        lane = lax.broadcasted_iota(jnp.int32, (TILE, TILE), 1)
        totals = jnp.zeros((TILE, TILE), F32)
        for head in range(heads):
            scores = dot_t(head_columns(queries, head, size), keys)
            scores = scores + bias_rows(table_ref, all_tiles[head], head, block)
            row_max = jnp.max(scores, axis=-1, keepdims=True)
            exponent = jnp.exp(scores - row_max)
            row_total = jnp.sum(exponent, axis=-1, keepdims=True)
            weights = (exponent * (1.0 / row_total)).astype(BF16)
            part = dot(weights, head_values[head])
            mixed = part if mixed is None else mixed + part
            totals = jnp.where(lane == head, row_max + jnp.log(row_total), totals)
        mixed_ref[rows, :] = mixed.astype(BF16)
        total_ref[rows, :] = totals


class Input:
    def __init__(self, copies, buffer):
        self.copies, self.buffer, self.shape = copies, buffer, buffer.shape
        self.begun, self.later = False, ()

    def begin(self):
        if not self.begun:
            for copy in self.copies:
                copy.start()
        self.begun = True

    def land(self):
        self.begin()
        for copy in self.copies:
            copy.wait()
        self.copies = ()
        for entry in self.later:
            entry.begin()
        self.later = ()

    def __getitem__(self, index):
        self.land()
        return self.buffer[index]


class Output:
    def __init__(self, copy, buffer):
        self.copy, self.buffer, self.shape, self.left = copy, buffer, buffer.shape, False

    def __getitem__(self, index):
        return self.buffer[index]

    def __setitem__(self, index, values):
        self.buffer[index] = values

    def leave(self):
        if not self.left:
            self.copy.start()
        self.left = True


def call(kernel, name, outs, smem, operands, scratch=(), first=None, limit=60, flops=10**5, moved=10**4):
    groups = [entry if isinstance(entry, tuple) else (entry,) for entry in operands]
    arrays = [array for group in groups for array in group]
    anywhere = pl.BlockSpec(memory_space=pl.ANY)
    held = [
        pltpu.VMEM((len(group),) * (len(group) > 1) + group[0].shape, group[0].dtype) for group in groups
    ] + [pltpu.VMEM(shape, kind) for shape, kind in outs]

    def body(*refs):
        refs = list(refs)

        def take(count):
            taken = refs[:count]
            del refs[:count]
            return taken

        scalars, sources, targets = take(len(smem)), take(len(arrays)), take(len(outs))
        in_buffers, out_buffers = take(len(groups)), take(len(outs))
        in_sems, out_sems = take(2)
        inputs, number = [], 0
        for group, buffer in zip(groups, in_buffers):
            copies = []
            for m in range(len(group)):
                place = buffer if len(group) == 1 else buffer.at[scalars[0][0, 0] ^ m]
                copies.append(pltpu.make_async_copy(sources[number], place, in_sems.at[number]))
                number += 1
            inputs.append(Input(copies, buffer))
        for entry in inputs[:first]:
            entry.begin()
            entry.later = inputs[len(inputs) if first is None else first :]
        outputs = [
            Output(pltpu.make_async_copy(buffer, target, out_sems.at[i]), buffer)
            for i, (buffer, target) in enumerate(zip(out_buffers, targets))
        ]
        kernel(*scalars, *inputs, *outputs, *refs)
        for entry in inputs:
            entry.land()
        for entry in outputs:
            entry.leave()
        for entry in outputs:
            entry.copy.wait()

    return pl.pallas_call(
        body,
        out_shape=tuple(jax.ShapeDtypeStruct(shape, kind) for shape, kind in outs),
        in_specs=[pl.BlockSpec(memory_space=pltpu.SMEM)] * len(smem) + [anywhere] * len(arrays),
        out_specs=(anywhere,) * len(outs),
        scratch_shapes=held
        + [pltpu.SemaphoreType.DMA((len(arrays),)), pltpu.SemaphoreType.DMA((len(outs),))]
        + [pltpu.VMEM(shape, kind) for shape, kind in scratch],
        compiler_params=pltpu.CompilerParams(vmem_limit_bytes=limit * MIB),
        cost_estimate=pl.CostEstimate(flops=flops, bytes_accessed=moved, transcendentals=0),
        name=name,
    )(*smem, *arrays)


def attend(tokens, gains, weights, table, heads):
    rows, columns = tokens.shape[0], weights[0].shape[0]
    small = ((rows, columns), BF16)
    return call(
        functools.partial(attend_kernel, heads, columns // heads),
        "attend",
        (small, small, small, small, ((rows, TILE), F32)),
        (table,),
        (tokens, gains, *weights),
    )


def hidden_kernel(tensor_ref, place_ref, tokens_ref, mixed_ref, weight_ref, gain_ref, router_ref, routes_ref, cot_ref, hidden_ref, own_ref, gate_ref, both):
    width = tokens_ref.shape[1]
    experts = router_ref.shape[0]
    gain = gain_ref[...].astype(F32).reshape(1, -1)
    for block in range(tokens_ref.shape[0] // TILE):
        rows = pl.ds(block * TILE, TILE)
        hidden = tokens_ref[rows, :].astype(F32)
        for m in range(TENSOR):
            hidden = hidden + dot(mixed_ref[m, rows, :], weight_ref[m])
        hidden_ref[rows, :] = hidden
        normed = (hidden * inv_rms_of(hidden) * gain).astype(BF16)
        probs = softmax(dot_t(normed, router_ref[...]))
        lane = lax.broadcasted_iota(jnp.int32, (TILE, experts), 1)
        gate = jnp.sum(jnp.where(lane == routes_ref[rows, :], probs, 0.0), axis=-1, keepdims=True)
        gate_ref[rows, :] = jnp.broadcast_to(gate, (TILE, TILE))
        both[rows, :width] = normed
        both[rows, width:] = (cot_ref[rows, :].astype(F32) * gate).astype(BF16)
    hidden_ref.leave()
    gate_ref.leave()
    slots = own_ref.shape[0]
    row = lax.broadcasted_iota(jnp.int32, (slots, place_ref.shape[1]), 0)
    own_ref[...] = dot((row == place_ref[...]).astype(BF16), both[...]).astype(BF16)


def softmax(values):
    exponent = jnp.exp(values - jnp.max(values, axis=-1, keepdims=True))
    return exponent / jnp.sum(exponent, axis=-1, keepdims=True)


def expert_kernel(me_ref, f_b, in_ref, b_b, out_ref, router_ref, f_a, b_a, keep_ref, send_ref, keep_r_ref, send_r_ref, active_ref, pre_ref, grad_ref):
    rows = f_a.shape[0]
    experts = router_ref.shape[0]
    lane = lax.broadcasted_iota(jnp.int32, (rows, experts), 1)
    own_hot = (lane == me_ref[0, 0]).astype(F32)
    total = None
    for place, (forward, backward) in enumerate(((f_b, b_b), (f_a, b_a))):
        pre = dot(forward[...], in_ref[...])
        square = pre * pre
        bent = jnp.tanh(GELU_SCALE * (pre + GELU_CUBE * square * pre))
        active = (0.5 * pre * (1.0 + bent)).astype(BF16)
        slope = 0.5 * (1.0 + bent) + 0.5 * pre * (1.0 - bent * bent) * (
            GELU_SCALE * (1.0 + 3.0 * GELU_CUBE * square)
        )
        grad_active = dot_t(backward[...], out_ref[...])
        grad_pre = (grad_active * slope).astype(BF16)
        gate_grad = jnp.sum(active.astype(F32) * grad_active, axis=1, keepdims=True)
        probs = softmax(dot_t(forward[...], router_ref[...]))
        grad_logits = (gate_grad * (own_hot - probs)).astype(BF16)
        back = dot_t(grad_pre, in_ref[...]) + dot(grad_logits, router_ref[...])
        where = pl.ds((1 - place) * rows, rows)
        active_ref[where, :] = active
        pre_ref[where, :] = grad_pre
        if place == 0:
            send_ref[...] = back.astype(BF16)
            send_ref.leave()
            send_r_ref[...] = dot(active, out_ref[...]).astype(BF16)
            send_r_ref.leave()
        else:
            keep_ref[...] = back
            keep_ref.leave()
            keep_r_ref[...] = dot(active, out_ref[...])
        part = t_dot(grad_logits, forward[...])
        total = part if total is None else total + part
    grad_ref[...] = total


def expert_pair(me, first, second, weight_in, weight_out, router):
    rows, width = first[0].shape
    hidden = weight_in.shape[1]
    return call(
        expert_kernel,
        "expert_pair",
        (
            ((rows, width), F32), ((rows, width), BF16), ((rows, width), F32), ((rows, width), BF16),
            ((2 * rows, hidden), BF16), ((2 * rows, hidden), BF16),
            (router.shape, F32),
        ),
        (me,),
        (second[0], weight_in, second[1], weight_out, router, *first),

    )


def expert_grad_kernel(f0, f1, f2, f3, b0, b1, b2, b3, active_a, active_b, pre_a, pre_b, in_ref, out_ref):
    rows = f0.shape[0]
    forward = jnp.concatenate([f0[...], f1[...], f2[...], f3[...]], axis=0)
    pre = jnp.concatenate([pre_a[...], pre_b[...]], axis=0)
    in_ref[...] = t_dot(forward, pre)
    backward = jnp.concatenate([b0[...], b1[...], b2[...], b3[...]], axis=0)
    active = jnp.concatenate([active_a[...], active_b[...]], axis=0)
    out_ref[...] = t_dot(active, backward)


def packed(rows, count):
    size = rows.shape[0] // count
    return jnp.concatenate([rows[n * size : (n + 1) * size] for n in range(count)], axis=1)


def unpacked(rows, count):
    size = rows.shape[1] // count
    return jnp.concatenate([rows[:, n * size : (n + 1) * size] for n in range(count)], axis=0)


def hidden_back_kernel(
    devices, place_ref, hidden_ref, r0, r1, r2, r3, cot_ref, gain_ref, wo_ref, mixed_ref,
    router_a, router_b, grad_ref, gm_ref, turned_ref, norm_ref, sums_ref, router_ref, attn_ref,
):
    tok_rows, width = hidden_ref.shape
    columns = mixed_ref.shape[1]
    chunk = r0.shape[0]
    gain = gain_ref[...].astype(F32).reshape(1, -1)
    norm_part = None
    for block in range(tok_rows // TILE):
        rows = pl.ds(block * TILE, TILE)
        place = place_ref[rows, :]
        back = None
        for m, returned in enumerate((r0, r1, r2, r3)):
            lane = lax.broadcasted_iota(jnp.int32, (TILE, chunk), 1) + m * chunk
            found = dot((lane == place).astype(BF16), returned[...])
            back = found if back is None else back + found
        hidden = hidden_ref[rows, :]
        inv = inv_rms_of(hidden)
        summed = jnp.sum((back * hidden * inv).reshape(TILE // 8, 8, width), axis=0)
        norm_part = summed if norm_part is None else norm_part + summed
        grad = cot_ref[rows, :].astype(F32) + rms_norm_back(hidden, inv, gain, back)
        grad_ref[rows, :] = grad
        low = grad.astype(BF16)
        attn_ref[rows, :] = low
        gm_ref[rows, :] = dot_t(low, wo_ref[...]).astype(BF16)
    grad_ref.leave()
    gm_ref.leave()
    unit = lax.broadcasted_iota(jnp.int32, (columns, columns), 0)
    unit = (unit == lax.broadcasted_iota(jnp.int32, (columns, columns), 1)).astype(BF16)
    sums = dot(dot_t(unit, mixed_ref[...]).astype(BF16), attn_ref[...]).T
    router = router_a[...] + router_b[...]
    router_ref[...] = router
    if devices == PAIRED:
        size = width // devices
        blocks = [packed(sums[n * size : (n + 1) * size], 4) for n in range(devices)]
        sums = jnp.concatenate([piece for block in blocks for piece in (block, router)], axis=0)
    sums_ref[...] = sums.astype(BF16)
    sums_ref.leave()
    turned_ref[...] = dot_t(wo_ref[...], attn_ref[...]).astype(BF16)
    norm_ref[...] = norm_part


def back_kernel(
    heads, size, devices, table_ref, core_ref, q_ref, k_ref, v_ref, gm_ref, turned_ref, total_ref,
    tokens_ref, gain_ref, wq_ref, wk_ref, wv_ref, norm_ref,
    sums_ref, keep_ref, send_ref, small_ref, back_t, turn_t, part_ref, normed_ref, qb_ref,
):
    tok_rows, width = tokens_ref.shape
    columns = q_ref.shape[1]
    count = LEN // TILE
    keys, all_values = k_ref[...], v_ref[...]
    back_t[...] = jnp.zeros_like(back_t)
    unit = lax.broadcasted_iota(jnp.int32, (columns, columns), 0)
    unit = (unit == lax.broadcasted_iota(jnp.int32, (columns, columns), 1)).astype(BF16)
    turn_t[pl.ds(0, columns), :] = dot_t(unit, q_ref[...]).astype(BF16)
    turn_t[pl.ds(columns, columns), :] = turned_ref[...]
    all_tiles = [bias_tiles(table_ref, head) for head in range(heads)]
    head_keys = [head_columns(keys, head, size) for head in range(heads)]
    near = [[None] * 3 for _ in range(heads)]
    far = [[None] * 2 for _ in range(heads)]
    for block in range(count):
        rows = pl.ds(block * TILE, TILE)
        queries, grads, totals = q_ref[rows, :], gm_ref[rows, :], total_ref[rows, :]
        query_back = None
        for head in range(heads):
            head_queries = head_columns(queries, head, size)
            head_grads = head_columns(grads, head, size)
            scores = dot_t(head_queries, keys)
            scores = scores + bias_rows(table_ref, all_tiles[head], head, block)
            probs = jnp.exp(scores - totals[:, head : head + 1])
            probs_grad = dot_t(head_grads, all_values)
            inner = jnp.sum(probs_grad * probs, axis=-1, keepdims=True)
            score_grad = (probs * (probs_grad - inner)).astype(BF16)
            part = dot(score_grad, head_keys[head])
            query_back = part if query_back is None else query_back + part
            mine = pl.ds(head * size, size)
            back_t[mine, :] += dot(turn_t[mine, rows], score_grad)
            mine = pl.ds(columns + head * size, size)
            back_t[mine, :] += dot(turn_t[mine, rows], probs.astype(BF16))
            wide = score_grad.astype(F32)
            for other in range(count):
                offset = other - block
                tile = wide[:, other * TILE : (other + 1) * TILE]
                if abs(offset) <= 1:
                    held = near[head][offset + 1]
                    near[head][offset + 1] = tile if held is None else held + tile
                else:
                    side = 0 if offset < 0 else 1
                    summed = jnp.sum(tile.reshape(TILE // 8, 8, TILE), axis=0)
                    held = far[head][side]
                    far[head][side] = summed if held is None else held + summed
        qb_ref[rows, :] = query_back.astype(BF16)
    inputs = tokens_ref[...].astype(F32)
    inv_first = inv_rms_of(inputs)
    normed_ref[...] = (inputs * inv_first * gain_ref[...].astype(F32).reshape(1, -1)).astype(BF16)
    query_back = qb_ref[...]
    key_t = back_t[pl.ds(0, columns), :].astype(BF16)
    value_t = back_t[pl.ds(columns, columns), :].astype(BF16)
    part_ref[...] = dot(query_back, wq_ref[...]) + t_dot(key_t, wk_ref[...]) + t_dot(value_t, wv_ref[...])
    half = tok_rows // 2
    core = core_ref[0, 0]
    keep_ref[...] = part_ref[pl.ds(pl.multiple_of(core * half, half), half), :]
    keep_ref.leave()
    send_ref[...] = part_ref[pl.ds(pl.multiple_of((1 - core) * half, half), half), :].astype(BF16)
    send_ref.leave()
    bias_row = jnp.concatenate([bias_sums(heads, near, far), jnp.zeros((8, width - TILE), F32)], axis=1)
    norm_row = jnp.broadcast_to(jnp.sum(norm_ref[...], axis=0, keepdims=True), (8, width))
    first_part = jnp.sum(part_ref[...] * tokens_ref[...].astype(F32) * inv_first, axis=0, keepdims=True)
    line = lax.broadcasted_iota(jnp.int32, (8, width), 0)
    lines = jnp.where(line == 0, first_part, jnp.where(line == 1, norm_row, jnp.where(line == 2, bias_row, 0.0)))
    small = lines
    small_ref[...] = small
    small_ref.leave()
    turned = (dot_t(unit, query_back).astype(BF16), key_t, value_t)
    parts = [dot(rows, normed_ref[...]) for rows in turned]
    sums = jnp.concatenate(parts, axis=0).T
    if devices == PAIRED:
        size = width // devices
        blocks = [sums[n * size : (n + 1) * size] for n in range(devices)]
        sums = jnp.concatenate(
            [
                piece
                for block in blocks
                for piece in (packed(block[:, : 2 * columns], 2), packed(block[:, 2 * columns :], 4), small)
            ],
            axis=0,
        )
    sums_ref[...] = sums.astype(BF16)
    sums_ref.leave()


def bias_sums(heads, near, far):
    upper = lax.broadcasted_iota(jnp.int32, (TILE, TILE), 1) >= lax.broadcasted_iota(jnp.int32, (TILE, TILE), 0)
    edges = tuple(range(8)) + (8,) + THRESHOLDS + (1 << 20,)
    lane = lax.broadcasted_iota(jnp.int32, (TILE, TILE), 0)
    place = lax.broadcasted_iota(jnp.int32, (TILE, TILE), 1)
    total = jnp.zeros((8, TILE), F32)

    def bucket(distance):
        found = jnp.zeros((TILE, TILE), jnp.int32)
        for n in range(1, 16):
            found = jnp.where(distance >= edges[n], n, found)
        return found

    for head in range(heads):
        before, here, beyond = near[head]
        start = head * BUCKETS
        ahead = diagonal_sums(jnp.where(upper, here, beyond))
        behind = diagonal_sums(jnp.where(upper, before, here))
        outside = (
            jnp.sum(jnp.where(upper, 0.0, before), axis=0, keepdims=True) + jnp.sum(far[head][0], axis=0, keepdims=True),
            jnp.sum(jnp.where(upper, beyond, 0.0), axis=0, keepdims=True) + jnp.sum(far[head][1], axis=0, keepdims=True),
        )
        targets = (
            start + jnp.where(lane == 0, 0, 16 + bucket(lane)),
            start + bucket(TILE - lane),
            jnp.full((TILE, TILE), start + 15, jnp.int32),
            jnp.full((TILE, TILE), start + 31, jnp.int32),
        )
        for row, target in zip((ahead, behind, *outside), targets):
            total = total + lax.dot_general(
                jnp.broadcast_to(row, (8, TILE)), (place == target).astype(F32), (((1,), (0,)), ((), ())),
                precision=lax.Precision.HIGHEST, preferred_element_type=F32,
            )
    return total


def swap(values, axis, mask):
    size = lax.axis_size(axis)
    return lax.ppermute(values, axis, [(i, i ^ mask) for i in range(size)])


def gather_tensor(values):
    far = swap(values, "tensor", 2)
    near = swap(values, "tensor", 1)
    return values, near, far, swap(far, "tensor", 1)


def exchange_expert(blocks):
    return lax.all_to_all(blocks, "expert", split_axis=0, concat_axis=0, tiled=True)


def after(values, done):
    return lax.optimization_barrier((values, done))[0]


def sum_expert(values):
    mask = 1
    while mask < lax.axis_size("expert"):
        values = values + swap(values, "expert", mask)
        mask = 2 * mask
    return values


def on_device(
    tokens,
    norm_first,
    w_query,
    w_key,
    w_value,
    w_output,
    bias_table,
    norm_second,
    w_router,
    w_expert_in,
    w_expert_out,
    routes,
    cotangent,
):
    tok_rows, width = tokens.shape
    experts = w_router.shape[1]
    capacity = max(2, 3 * tok_rows // (2 * experts))
    quarter = -(-capacity // TENSOR)
    heads_here = bias_table.shape[1]
    columns = w_query.shape[1]
    chunk_rows = experts * quarter
    half = tok_rows // 2
    devices = lax.axis_size("expert")
    paired = devices == PAIRED
    my_tensor = lax.axis_index("tensor")
    my_expert = lax.axis_index("expert").astype(jnp.int32).reshape(1, 1)
    core = (my_tensor & 1).astype(jnp.int32)
    weight_in = w_expert_in[0]
    weight_out = w_expert_out[0]
    router = w_router.T
    weights = (w_query.T, w_key.T, w_value.T)
    table = bias_table.T.astype(F32)

    queries, keys, values, mixed, totals = attend(tokens, norm_first, weights, table, heads_here)

    chosen = routes[:, 0]
    route_hot = chosen[:, None] == jnp.arange(experts, dtype=jnp.int32)[None, :]
    places = jnp.arange(tok_rows, dtype=jnp.int32)
    before = (places[:, None] > places[None, :]).astype(BF16)
    earlier = dot(before, route_hot.astype(BF16))
    slot_index = jnp.sum(jnp.where(route_hot, earlier, 0.0), axis=1).astype(jnp.int32)
    chunk = (slot_index // quarter) ^ my_tensor
    place = (chunk * experts + chosen) * quarter + slot_index % quarter

    output_parts = gather_tensor(w_output)
    hidden, own, gate = call(
        hidden_kernel,
        "hidden",
        (((tok_rows, width), F32), ((chunk_rows, 2 * width), BF16), ((tok_rows, TILE), F32)),
        (my_tensor.astype(jnp.int32).reshape(1, 1),),
        (
            place[None, :], tokens, gather_tensor(after(mixed, output_parts[2])), output_parts, norm_second, router,
            routes, cotangent,
        ),
        scratch=(((tok_rows, 2 * width), BF16),),
    )
    arrived = exchange_expert(own.reshape(experts, quarter, 2 * width)).reshape(chunk_rows, 2 * width)
    forward, backward = arrived[:, :width], arrived[:, width:]
    forward_far, backward_far = swap(forward, "tensor", 2), swap(backward, "tensor", 2)
    forward_near, backward_near = swap(forward, "tensor", 1), swap(backward, "tensor", 1)

    keep_a, send_a, kept_result, send_result, active_a, pre_a, router_a = expert_pair(
        my_expert, (forward, backward), (forward_near, backward_near), weight_in, weight_out, router
    )
    forward_diag = swap(after(forward_far, active_a), "tensor", 1)
    backward_diag = swap(after(backward_far, active_a), "tensor", 1)
    got_a = swap(send_a, "tensor", 1)
    keep_b, send_b, far_result, far_send, active_b, pre_b, router_b = expert_pair(
        my_expert, (forward_far, backward_far), (forward_diag, backward_diag), weight_in, weight_out, router
    )
    other = (keep_b + swap(send_b, "tensor", 1).astype(F32)).astype(BF16)
    other_back = swap(other, "tensor", 2)

    own_back = ((keep_a + got_a.astype(F32)) + other_back.astype(F32)).astype(BF16)
    home = exchange_expert(own_back.reshape(experts, quarter, width)).reshape(chunk_rows, width)

    far_result = (far_result + swap(after(far_send, other), "tensor", 1).astype(F32)).astype(BF16)
    kept_result = kept_result + swap(after(send_result, other), "tensor", 1).astype(F32)
    other_result = swap(after(far_result, own_back), "tensor", 2)
    grad_expert_in, grad_expert_out = call(
        expert_grad_kernel,
        "expert_grads",
        ((weight_in.shape, F32), (weight_out.shape, F32)),
        (),
        (
            forward, forward_near, forward_far, forward_diag, backward, backward_near, backward_far, backward_diag,
            after(active_a, own_back), active_b, pre_a, pre_b,
        ),
    )
    own_result = (kept_result + other_result.astype(F32)).astype(BF16)
    home = after(home, (own_result, grad_expert_in))
    home_far = swap(home, "tensor", 2)
    returned_back = (home, swap(home, "tensor", 1), home_far, swap(home_far, "tensor", 1))

    result = exchange_expert(after(own_result, home).reshape(experts, quarter, width)).reshape(chunk_rows, width)

    grad_hidden, grad_mixed, turned, norm_part, output_sums, router_part = call(
        functools.partial(hidden_back_kernel, devices),
        "hidden_back",
        (
            ((tok_rows, width), F32), ((tok_rows, columns), BF16), ((columns, tok_rows), BF16), ((8, width), F32),
            ((width // 4 + devices * experts, 4 * columns) if paired else (width, columns), BF16),
            (router.shape, F32),
        ),
        (),
        (place[:, None], hidden, *returned_back, cotangent, norm_second, w_output, mixed, router_a, router_b),
        first=9,
        scratch=(((tok_rows, width), BF16),),
    )

    grad_hidden, grad_mixed, turned, norm_part, output_sums, _ = lax.optimization_barrier(
        (grad_hidden, grad_mixed, turned, norm_part, output_sums, result)
    )

    output_sums = exchange_expert(output_sums.reshape(devices, -1, output_sums.shape[1]))
    result_far = swap(result, "tensor", 2)
    sums, keep, send, small = call(
        functools.partial(back_kernel, heads_here, columns // heads_here, devices),
        "layer_back",
        (
            ((3 * width // 4 + devices * 8, 4 * columns) if paired else (width, 3 * columns), BF16),
            ((half, width), F32), ((half, width), BF16), ((8, width), F32),
        ),
        (table, core.reshape(1, 1)),
        (
            queries, keys, values, grad_mixed, turned, totals, tokens, norm_first, *weights, norm_part,
        ),
        first=6,
        scratch=(
            ((2 * columns, tok_rows), F32), ((2 * columns, tok_rows), BF16), ((tok_rows, width), F32),
            ((tok_rows, width), BF16), ((tok_rows, columns), BF16),
        ),
    )
    sums, keep, send, small = lax.optimization_barrier((sums, keep, send, small, output_sums, result_far))[:4]

    sums = exchange_expert(sums.reshape(devices, -1, sums.shape[1]))

    pair = (keep + swap(send, "tensor", 1).astype(F32)).astype(BF16)
    total = (pair.astype(F32) + swap(pair, "tensor", 2).astype(F32)).astype(BF16)

    grads = jnp.sum(sums.astype(F32), axis=0)
    grad_output = jnp.sum(output_sums.astype(F32), axis=0)
    if paired:
        split = width // PAIRED // 2
        small = grads[3 * split // 2 :]
        grads = jnp.concatenate([unpacked(grads[:split], 2), unpacked(grads[split : 3 * split // 2], 4)], axis=1)
        grad_router = grad_output[split // 2 :]
        grad_output = unpacked(grad_output[: split // 2], 4)
    else:
        small = sum_expert(small)
        grad_router = sum_expert(router_part)

    near = swap(total, "tensor", 1)
    low = jnp.where(core == 1, near, total).astype(F32)
    high = jnp.where(core == 1, total, near).astype(F32)
    normed_back = jnp.concatenate([low, high])
    inputs = tokens.astype(F32)
    grad_tokens = grad_hidden + rms_norm_back(
        inputs, inv_rms_of(inputs), norm_first.astype(F32)[None, :], normed_back
    )

    returned = (result, swap(after(result, total), "tensor", 1), result_far, swap(result_far, "tensor", 1))
    place_hot = (
        place[:, None] == jnp.arange(TENSOR * chunk_rows, dtype=jnp.int32)[None, :]
    ).astype(BF16)
    layer_out = (hidden + gate[:, :1] * dot(place_hot, jnp.concatenate(returned))).astype(BF16)

    grad_router = grad_router + swap(after(grad_router, total), "tensor", 1)
    grad_router = grad_router + swap(grad_router, "tensor", 2)
    first = small + swap(small, "tensor", 1)
    first = first + swap(after(first, (result_far, grad_router)), "tensor", 2)
    bias_size = BUCKETS * heads_here
    return (
        layer_out,
        grad_tokens,
        first[0],
        grads[:, :columns],
        grads[:, columns : 2 * columns],
        grads[:, 2 * columns :],
        grad_output.T,
        small[2, :bias_size].reshape(heads_here, BUCKETS).T,
        small[1],
        grad_router.T,
        grad_expert_in[None],
        grad_expert_out[None],
    )


def solution(mesh):
    return jax.shard_map(
        on_device,
        mesh=mesh,
        in_specs=(
            P("expert", None),
            P(),
            P(None, "tensor"),
            P(None, "tensor"),
            P(None, "tensor"),
            P("tensor", None),
            P(None, "tensor"),
            P(),
            P(),
            P("expert", None, "tensor"),
            P("expert", "tensor", None),
            P("expert", None),
            P("expert", None),
        ),
        out_specs=(
            P("expert", None),
            P("expert", None),
            P(),
            P("expert", "tensor"),
            P("expert", "tensor"),
            P("expert", "tensor"),
            P("tensor", "expert"),
            P(None, "tensor"),
            P(),
            P(),
            P("expert", None, "tensor"),
            P("expert", "tensor", None),
        ),
        check_vma=False,
    )
```
